32 devices in a mesh: shot: 16 (over z, x, core), dom: 2 (over y).
Axes of the slice: x: 2, y: 2, z: 4, core: 2. Of those that a mesh axis runs over, the one named last changes fastest.
Arguments:
- velocity: float32 [16, 128, 256], P('dom', 'shot'), may hold values from 0.15 to 0.4
- epsilon: float32 [16, 128, 256], P('dom', 'shot'), may hold values from 0.05 to 0.3
- forward_state: float32 [16, 4, 16, 128, 256], P('shot', None, 'dom'), may hold values from -1.2 to 1.2
- adjoint_state: float32 [16, 4, 16, 128, 256], P('shot', None, 'dom'), may hold values from -1.2 to 1.2
- source_cell: int32 [16], P('shot'), may hold values from 0 to 524287
- wavelet: float32 [16, 3], P('shot'), may hold values from -6 to 6
- receiver_cells: int32 [16, 256], P('shot'), may hold values from 0 to 524287
- residuals: float32 [16, 4, 256], P('shot'), may hold values from -6 to 6
Outputs:
- velocity_grad: float32 [16, 128, 256], P('dom', 'shot')
- epsilon_grad: float32 [16, 128, 256], P('dom', 'shot')
The draws below stay inside these ranges and needn't reach their ends.
Inputs may be any that keep to these rules, and one draw needn't show every extreme that they name: `source_cell`: flat grid cell index (z * 128 + x) * 256 + y of each shot's source. `receiver_cells`: flat grid cell indices (z * 128 + x) * 256 + y of each shot's receivers; two receivers may share a cell.
All inputs are finite; a program needn't handle non-finite values.
Results may differ from the reference program's by a relative error of at most 0.00002.
Values sent between devices are 32-bit elements; how exact they have to be, the bound alone decides.
A program may use at most 128 MiB of HBM per device.

```python
import math
import jax
import jax.numpy as jnp
from jax import lax

NX = 128
NY = 256
NREC = 256
STEPS = 4
SHOTS = 16
NZ = 16


def place_ends(drawn, rng, smallest, largest):
    shape = drawn.shape
    place = [jax.random.randint(jax.random.fold_in(rng, axis), (), 0, shape[axis]) for axis in range(len(shape))]
    drawn = drawn.at[tuple(place)].set(smallest)
    longest = shape.index(max(shape))
    place[longest] = (place[longest] + 1) % shape[longest]
    return drawn.at[tuple(place)].set(largest)


def level_of(rng, extent, pieces, least, largest):
    level = 1.0
    for dim, parts in pieces:
        heights = jax.random.uniform(jax.random.fold_in(jax.random.fold_in(rng, 6), dim), (parts,), jnp.float32, least / len(pieces), largest / len(pieces))
        level = level * jnp.repeat(jnp.exp(heights), extent[dim] // parts).reshape((-1,) + (1,) * (len(extent) - 1 - dim))
    return level


def centred(key, shape, spread, limit, pieces=(), dtype=jnp.bfloat16):
    result = jax.random.normal(key, shape, jnp.float32) * spread
    if len(pieces) > 0:
        result = level_of(key, shape, pieces, -0.22, 0.18) * result
    return jnp.clip(result, min=-limit, max=limit).astype(dtype)


def setup_inputs(seed: int = 0) -> dict:
    splits = jax.random.split(jax.random.key(seed), 9)
    return {
        "velocity": jnp.clip(jnp.exp(math.log(0.4) - 0.98082923 * jax.random.uniform(splits[0], (NZ, NX, NY), jnp.float32) ** level_of(splits[0], (NZ, NX, NY), ((0, 2), (1, 16)), -0.2, 0.2)), 0.15, 0.4),
        "epsilon": jnp.clip(jnp.exp(math.log(0.3) - 1.7917595 * jax.random.uniform(splits[1], (NZ, NX, NY), jnp.float32) ** level_of(splits[1], (NZ, NX, NY), ((0, 2), (1, 16)), -0.2, 0.2)), 0.05, 0.3),
        "forward_state": centred(splits[2], (SHOTS, 4, NZ, NX, NY), 0.2, 1.2, ((0, 16), (2, 2)), jnp.float32),
        "adjoint_state": centred(splits[3], (SHOTS, 4, NZ, NX, NY), 0.2, 1.2, ((0, 16), (2, 2)), jnp.float32),
        "source_cell": place_ends(jax.random.randint(splits[4], (SHOTS,), 0, NZ * NX * NY), jax.random.fold_in(splits[4], 1), 0, (NZ * NX * NY) - 1).astype(jnp.int32),
        "wavelet": centred(splits[5], (SHOTS, STEPS - 1), 1.0, 6.0, ((0, 16),), jnp.float32),
        "receiver_cells": place_ends(jax.random.randint(splits[6], (SHOTS, NREC), 0, NZ * NX * NY), jax.random.fold_in(splits[6], 1), 0, (NZ * NX * NY) - 1).astype(jnp.int32),
        "residuals": centred(splits[7], (SHOTS, STEPS, NREC), 1.0, 6.0, ((0, 16),), jnp.float32),
    }


def stencil(padded, axis, size):
    def part(offset):
        return lax.slice_in_dim(padded, offset, offset + size, axis=axis)
    return (4.0 / 3.0) * (part(1) + part(3)) - (1.0 / 12.0) * (part(0) + part(4)) - 2.5 * part(2)


def second_diff(field, axis):
    widths = [(0, 0), (0, 0), (0, 0)]
    widths[axis] = (2, 2)
    return stencil(jnp.pad(field, widths), axis, field.shape[axis])


def lateral(field):
    return second_diff(field, 1) + second_diff(field, 2)


def inject(field, cell_ids, amounts):
    return field.reshape(-1).at[cell_ids].add(amounts).reshape(field.shape)


def reference(velocity, epsilon, forward_state, adjoint_state, source_cell, wavelet, receiver_cells, residuals):
    stiffness = velocity * velocity
    stretch = 1.0 + 2.0 * epsilon

    def one_shot(carry, item):
        fstate, astate, source, pulses, receivers, traces = item
        pressure_old, pressure_now, support_old, support_now = fstate[0], fstate[1], fstate[2], fstate[3]
        flat_terms = []
        depth_terms = []
        for moment in range(STEPS):
            flat_term = lateral(pressure_now)
            depth_term = second_diff(support_now, 0)
            flat_terms.append(flat_term)
            depth_terms.append(depth_term)
            if moment + 1 < STEPS:
                pressure_new = 2.0 * pressure_now - pressure_old + stiffness * (stretch * flat_term + depth_term)
                support_new = 2.0 * support_now - support_old + stiffness * (flat_term + depth_term)
                pressure_new = inject(pressure_new, source, pulses[moment])
                support_new = inject(support_new, source, pulses[moment])
                pressure_old, pressure_now = pressure_now, pressure_new
                support_old, support_now = support_now, support_new
        back_old, back_now, side_old, side_now = astate[0], astate[1], astate[2], astate[3]
        image_one = jnp.zeros_like(velocity)
        image_two = jnp.zeros_like(velocity)
        for moment in reversed(range(STEPS)):
            back_new = 2.0 * back_now - back_old + lateral(stiffness * (stretch * back_now + side_now))
            back_new = inject(back_new, receivers, traces[moment])
            side_new = 2.0 * side_now - side_old + second_diff(stiffness * (back_now + side_now), 0)
            image_one = image_one + back_new * flat_terms[moment]
            image_two = image_two + back_new * depth_terms[moment] + side_new * (flat_terms[moment] + depth_terms[moment])
            back_old, back_now = back_now, back_new
            side_old, side_now = side_now, side_new
        return (carry[0] + image_one, carry[1] + image_two), None

    start = (jnp.zeros_like(velocity), jnp.zeros_like(velocity))
    totals, unused = lax.scan(one_shot, start, (forward_state, adjoint_state, source_cell, wavelet, receiver_cells, residuals))
    velocity_grad = 2.0 * velocity * (stretch * totals[0] + totals[1])
    epsilon_grad = 2.0 * stiffness * totals[0]
    return velocity_grad, epsilon_grad
```

```python
import functools

import jax
import jax.numpy as jnp
from jax import lax
from jax.experimental import pallas as pl
from jax.experimental.pallas import tpu as pltpu
from jax.sharding import PartitionSpec as P

STEPS = 4
PAD = 8
LANES = 128
C1, C2 = 4.0 / 3.0, 1.0 / 12.0
MESH = pl.DeviceIdType.MESH


def kernel(
    shots, doms, chunk,
    vel, eps, fwd, adj, src, wav, rec, res, out_vel, out_eps,
    p0, p1, q0, q1, w0, w1, s0, s1, a0, a1, a2, b0, b1, b2,
    flat0, flat1, dep0, dep1, img1, img2, stiff, stretch, inj, hot,
    gath, term, from_core, from_x, from_z,
    load_sem, own_sem, z_send, x_send, c_send, g_recv,
    halo_send, halo_recv, rc_send, rc_recv, rx_send, rx_recv, rz_send, rz_recv,
):
    depth, width, length = stiff.shape
    rows = vel.shape[1]
    nrec = rec.shape[1]
    zs = shots // 4
    me = lax.axis_index("shot")
    dom = lax.axis_index("dom")
    core = lax.rem(me, 2)
    xi = lax.rem(me // 2, 2)
    zi = me // 4
    n_chunks = width // chunk

    def shot_at(z, x, c):
        return (z * 2 + x) * 2 + c

    has_low = dom > 0
    has_high = dom < doms - 1

    loads = []

    def load(source, target):
        copy = pltpu.make_async_copy(source, target, load_sem.at[len(loads)])
        copy.start()
        loads.append(copy)

    own = [
        pltpu.make_async_copy(vel, gath.at[me, 0], own_sem.at[0]),
        pltpu.make_async_copy(eps, gath.at[me, 1], own_sem.at[1]),
    ]
    for copy in own:
        copy.start()
    inner = pl.ds(PAD, width)
    cells = pl.ds(2, depth)
    load(adj.at[0, 1], a1)
    load(adj.at[0, 3], b1)
    load(fwd.at[0, 1], p1.at[:, inner, :])
    load(fwd.at[0, 3], q1.at[cells])
    load(fwd.at[0, 0], p0.at[:, inner, :])
    load(fwd.at[0, 2], q0.at[cells])
    load(adj.at[0, 0], a0)
    load(adj.at[0, 2], b0)

    barrier = pltpu.get_barrier_semaphore()
    for d in range(1, zs):
        pl.semaphore_signal(
            barrier, inc=1, device_id={"shot": shot_at(lax.rem(zi + d, zs), xi, core)},
            device_id_type=MESH)
    pl.semaphore_signal(
        barrier, inc=1, device_id={"shot": shot_at(zi, 1 - xi, core)}, device_id_type=MESH)
    pl.semaphore_signal(
        barrier, inc=1, device_id={"shot": shot_at(zi, xi, 1 - core)}, device_id_type=MESH)

    @pl.when(has_low)
    def _():
        pl.semaphore_signal(barrier, inc=1, device_id={"dom": dom - 1}, device_id_type=MESH)

    @pl.when(has_high)
    def _():
        pl.semaphore_signal(barrier, inc=1, device_id={"dom": dom + 1}, device_id_type=MESH)

    beside = jnp.where(has_low, 1, 0) + jnp.where(has_high, 1, 0)
    pl.semaphore_wait(barrier, zs + 1 + beside)

    def low_copy(source, field, slot):
        return pltpu.make_async_remote_copy(
            src_ref=source, dst_ref=field.at[pl.ds(depth + 2, 2)],
            send_sem=halo_send.at[slot, 0], recv_sem=halo_recv.at[slot, 1],
            device_id={"dom": dom - 1}, device_id_type=MESH)

    def high_copy(source, field, slot):
        return pltpu.make_async_remote_copy(
            src_ref=source, dst_ref=field.at[pl.ds(0, 2)],
            send_sem=halo_send.at[slot, 1], recv_sem=halo_recv.at[slot, 0],
            device_id={"dom": dom + 1}, device_id_type=MESH)

    def send_halo(field, slot, low=None, high=None):
        low = field.at[pl.ds(2, 2)] if low is None else low
        high = field.at[pl.ds(depth, 2)] if high is None else high

        @pl.when(has_low)
        def _():
            low_copy(low, field, slot).start()

        @pl.when(has_high)
        def _():
            high_copy(high, field, slot).start()

    def wait_halo(field, slot):
        @pl.when(has_low)
        def _():
            low_copy(field.at[pl.ds(2, 2)], field, slot).wait_send()
            high_copy(field.at[pl.ds(depth, 2)], field, slot).wait_recv()

        @pl.when(has_high)
        def _():
            high_copy(field.at[pl.ds(depth, 2)], field, slot).wait_send()
            low_copy(field.at[pl.ds(2, 2)], field, slot).wait_recv()

    send_halo(q1, 0, fwd.at[0, 3, pl.ds(0, 2)], fwd.at[0, 3, pl.ds(depth - 2, 2)])

    def block_copy(owner, target, send_sem):
        return pltpu.make_async_remote_copy(
            src_ref=gath.at[owner], dst_ref=gath.at[owner],
            send_sem=send_sem, recv_sem=g_recv.at[owner],
            device_id={"shot": target}, device_id_type=MESH)

    def to_x(z):
        return block_copy(shot_at(z, xi, core), shot_at(zi, 1 - xi, core), x_send.at[z])

    def to_core(z, x):
        return block_copy(
            shot_at(z, x, core), shot_at(zi, xi, 1 - core), c_send.at[z * 2 + x])

    def to_z(d):
        return block_copy(me, shot_at(lax.rem(zi + d, zs), xi, core), z_send.at[d])

    def arrived(owner):
        block_copy(owner, me, x_send.at[0]).wait_recv()

    for copy in own:
        copy.wait()
    to_x(zi).start()
    for d in range(1, zs):
        to_z(d).start()
    to_core(zi, xi).start()

    edge = jnp.zeros((depth, PAD, length), jnp.float32)
    for field in (p0, p1, w0, w1):
        field[:, 0:PAD, :] = edge
        field[:, PAD + width:PAD + width + PAD, :] = edge
    halo = jnp.zeros((2, width, length), jnp.float32)

    @pl.when(dom == 0)
    def _():
        for field in (q0, q1, s0, s1):
            field[0:2] = halo

    @pl.when(dom == doms - 1)
    def _():
        for field in (q0, q1, s0, s1):
            field[depth + 2:depth + 4] = halo

    first_row = dom * (depth * width)
    rec_row = rec[...] // length - first_row
    rec_col = lax.rem(rec[...], length)
    all_rows = depth * width

    def fill_hot(z, carry):
        ids = lax.broadcasted_iota(jnp.int32, (width, nrec), 0) + z * width
        hot[pl.ds(pl.multiple_of(z * width, width), width), :] = jnp.where(
            ids == rec_row, 1.0, 0.0).astype(jnp.bfloat16)
        return carry

    def inject_moment(k):
        col_hit = lax.broadcasted_iota(jnp.int32, (length, nrec), 0) == rec_col
        amount = res[0, k:k + 1, :]
        parts = []
        for _ in range(3):
            part = amount.astype(jnp.bfloat16).astype(jnp.float32)
            parts.append(jnp.where(col_hit, part, 0.0).astype(jnp.bfloat16))
            amount = amount - part

        def fill(z, carry):
            here = hot[pl.ds(pl.multiple_of(z * width, width), width), :]
            total = None
            for part in parts:
                product = lax.dot_general(
                    here, part, (((1,), (1,)), ((), ())),
                    preferred_element_type=jnp.float32)
                total = product if total is None else total + product
            inj[k, z] = total
            return carry

        lax.fori_loop(0, depth, fill, 0)

    lax.fori_loop(0, depth, fill_hot, 0)
    thunks = [functools.partial(inject_moment, k) for k in range(STEPS)]
    for d in range(1, zs):
        if thunks:
            thunks.pop(0)()
        other = lax.rem(zi + (zs - d), zs)
        arrived(shot_at(other, xi, core))
        to_x(other).start()
        to_core(other, xi).start()
    for thunk in thunks:
        thunk()
    for d in range(zs):
        other = lax.rem(zi + (zs - d), zs)
        arrived(shot_at(other, 1 - xi, core))
        to_core(other, 1 - xi).start()
    for copy in loads:
        copy.wait()
    for z in range(zs):
        for x in range(2):
            arrived(shot_at(z, x, 1 - core))
    for d in range(1, zs):
        to_z(d).wait_send()
    for z in range(zs):
        to_x(z).wait_send()
        for x in range(2):
            to_core(z, x).wait_send()
    for s in range(shots):
        speed = gath[s, 0]
        stiff[:, s * rows:(s + 1) * rows, :] = speed * speed
        stretch[:, s * rows:(s + 1) * rows, :] = 1.0 + 2.0 * gath[s, 1]

    lane = lax.broadcasted_iota(jnp.int32, (chunk, LANES), 1)

    def along_y(field):
        tiles = [field[:, t:t + LANES] for t in range(0, length, LANES)]

        def shifted(amount):
            turned = [pltpu.roll(t, amount % LANES, 1) for t in tiles]
            result = []
            for i in range(len(tiles)):
                if amount > 0:
                    fill = turned[i - 1] if i > 0 else 0.0
                    result.append(jnp.where(lane >= amount, turned[i], fill))
                else:
                    fill = turned[i + 1] if i + 1 < len(tiles) else 0.0
                    result.append(jnp.where(lane < LANES + amount, turned[i], fill))
            return jnp.concatenate(result, axis=1)

        return shifted(1) + shifted(-1), shifted(2) + shifted(-2)

    def lateral(field, z, r0):
        window = field[z, pl.ds(r0, chunk + 2 * PAD), :]

        def at(offset):
            turned = pltpu.roll(window, -offset % (chunk + 2 * PAD), 0)
            return turned[PAD:PAD + chunk]

        centre = window[PAD:PAD + chunk]
        near, far = along_y(centre)
        near = near + (at(1) + at(-1))
        far = far + (at(2) + at(-2))
        return centre, C1 * near - C2 * far - 5.0 * centre

    def vertical(field, z, r0):
        def at(offset):
            return field[z + (2 + offset), pl.ds(r0, chunk), :]

        centre = at(0)
        return centre, C1 * (at(1) + at(-1)) - C2 * (at(2) + at(-2)) - 2.5 * centre

    source_row = src[0] // length - first_row
    source_col = lax.rem(src[0], length)
    row_ids = lax.broadcasted_iota(jnp.int32, (chunk, length), 0)
    col_ids = lax.broadcasted_iota(jnp.int32, (chunk, length), 1)
    P_, Q_ = (p0, p1), (q0, q1)
    W_, S_ = (w0, w1), (s0, s1)

    def forward(k, z, r0):
        now, old = (k + 1) % 2, k % 2
        here = (z, pl.ds(r0, chunk), slice(None))
        p_now, flat = lateral(P_[now], z, r0)
        q_now, dep = vertical(Q_[now], z, r0)
        if k + 1 < STEPS:
            st, sr = stiff[here], stretch[here]
            hit = (row_ids == source_row - (z * width + r0)) & (col_ids == source_col)
            pulse = jnp.where(hit, wav[0, k], 0.0)
            inside = (z, pl.ds(r0 + PAD, chunk), slice(None))
            layer = (z + 2, pl.ds(r0, chunk), slice(None))
            P_[old][inside] = 2.0 * p_now - P_[old][inside] + st * (sr * flat + dep) + pulse
            Q_[old][layer] = 2.0 * q_now - Q_[old][layer] + st * (flat + dep) + pulse
        if k == 0:
            flat0[here], dep0[here] = flat, dep
        elif k == 1:
            flat1[here], dep1[here] = flat, dep
        elif k == 2:
            a, b = a1[here], b1[here]
            img1[here] = a * flat
            img2[here] = a * dep + b * (flat + dep)
        else:
            a, b = a0[here], b0[here]
            img1[here] = img1[here] + a * flat
            img2[here] = img2[here] + (a * dep + b * (flat + dep))

    def weigh(slot, z, r0, a, b):
        here = (z, pl.ds(r0, chunk), slice(None))
        st, sr = stiff[here], stretch[here]
        W_[slot][z, pl.ds(r0 + PAD, chunk), :] = st * (sr * a + b)
        S_[slot][z + 2, pl.ds(r0, chunk), :] = st * (a + b)

    def start_adjoint(z, r0):
        here = (z, pl.ds(r0, chunk), slice(None))
        weigh(0, z, r0, a1[here], b1[here])

    def adjoint(k, z, r0):
        turn = STEPS - 1 - k
        old_a, now_a, new_a = ((a0, a1, a0), (a1, a0, a1), (a0, a1, a2), (a1, a2, None))[turn]
        old_b, now_b, new_b = ((b0, b1, b0), (b1, b0, b1), (b0, b1, b2), (b1, b2, None))[turn]
        here = (z, pl.ds(r0, chunk), slice(None))
        a = 2.0 * now_a[here] - old_a[here] + lateral(W_[turn % 2], z, r0)[1] + inj[(k,) + here]
        b = 2.0 * now_b[here] - old_b[here] + vertical(S_[turn % 2], z, r0)[1]
        if new_a is not None:
            new_a[here], new_b[here] = a, b
            weigh((turn + 1) % 2, z, r0, a, b)
        if k == 1:
            flat, dep = flat1[here], dep1[here]
            img1[here] = img1[here] + a * flat
            img2[here] = img2[here] + (a * dep + b * (flat + dep))
        elif k == 0:
            flat, dep = flat0[here], dep0[here]
            one = img1[here] + a * flat
            two = img2[here] + (a * dep + b * (flat + dep))
            st, sr = stiff[here], stretch[here]
            for i in range(chunk // rows):
                part = slice(i * rows, (i + 1) * rows)
                d = r0 // rows + i
                speed = gath[d, 0, z]
                term[d, 0, z] = 2.0 * speed * (sr[part] * one[part] + two[part])
                term[d, 1, z] = 2.0 * st[part] * one[part]

    def sweep(body, outer):
        count = 4 if outer else depth - 4

        def turn(i, carry):
            j = i // n_chunks
            z = j + (j // 2) * (depth - 4) if outer else j + 2
            body(z, pl.multiple_of(lax.rem(i, n_chunks) * chunk, chunk))
            return carry

        lax.fori_loop(0, count * n_chunks, turn, 0)

    sweep(start_adjoint, True)
    send_halo(s0, 4)
    wait_halo(q1, 0)
    sweep(functools.partial(forward, 0), True)
    send_halo(q0, 1)
    sweep(start_adjoint, False)
    sweep(functools.partial(forward, 0), False)
    for turn in range(STEPS - 1):
        k = STEPS - 1 - turn
        wait_halo(S_[turn % 2], 4 + turn)
        sweep(functools.partial(adjoint, k), True)
        send_halo(S_[(turn + 1) % 2], 5 + turn)
        sweep(functools.partial(adjoint, k), False)
        f = turn + 1
        wait_halo(Q_[(f + 1) % 2], f)
        sweep(functools.partial(forward, f), True)
        if f + 1 < STEPS:
            send_halo(Q_[f % 2], f + 1)
        sweep(functools.partial(forward, f), False)
    wait_halo(S_[(STEPS - 1) % 2], 3 + STEPS)

    def core_sum(j):
        return pltpu.make_async_remote_copy(
            src_ref=term.at[2 * j + (1 - core)], dst_ref=from_core.at[j],
            send_sem=rc_send.at[j], recv_sem=rc_recv.at[j],
            device_id={"shot": shot_at(zi, xi, 1 - core)}, device_id_type=MESH)

    def x_sum(z):
        return pltpu.make_async_remote_copy(
            src_ref=term.at[shot_at(z, 1 - xi, core)], dst_ref=from_x.at[z],
            send_sem=rx_send.at[z], recv_sem=rx_recv.at[z],
            device_id={"shot": shot_at(zi, 1 - xi, core)}, device_id_type=MESH)

    def z_sum(d):
        z = lax.rem(zi + d, zs)
        return pltpu.make_async_remote_copy(
            src_ref=term.at[shot_at(z, xi, core)], dst_ref=from_z.at[d],
            send_sem=rz_send.at[d], recv_sem=rz_recv.at[d],
            device_id={"shot": shot_at(z, xi, core)}, device_id_type=MESH)

    pairs = chunk // rows // 2

    def last(c, carry):
        r0 = pl.multiple_of(c * chunk, chunk)

        def layer(z, inner_carry):
            adjoint(0, z, r0)
            return inner_carry

        lax.fori_loop(0, depth, layer, 0)
        for i in range(pairs):
            core_sum(c * pairs + i).start()
        return carry

    lax.fori_loop(0, n_chunks, last, 0)

    def add(owner, arriving):
        term[owner] = term[owner] + arriving

    order = list(range(1, zs)) + [0]
    for d in order:
        z = lax.rem(zi + d, zs)
        j = z * 2 + (1 - xi)
        core_sum(j).wait_recv()
        add(2 * j + core, from_core[j])
        x_sum(z).start()
    for d in order:
        z = lax.rem(zi + d, zs)
        j = z * 2 + xi
        core_sum(j).wait_recv()
        add(2 * j + core, from_core[j])
    for d in order:
        z = lax.rem(zi + d, zs)
        x_sum(z).wait_recv()
        add(shot_at(z, xi, core), from_x[z])
        if d > 0:
            z_sum(d).start()
    total = term[me]
    for d in range(1, zs):
        z_sum(d).wait_recv()
        total = total + from_z[d]
    out_vel[...] = total[0]
    out_eps[...] = total[1]
    for j in range(2 * zs):
        core_sum(j).wait_send()
    for z in range(zs):
        x_sum(z).wait_send()
    for d in range(1, zs):
        z_sum(d).wait_send()


def on_device(velocity, epsilon, forward_state, adjoint_state, source_cell, wavelet,
              receiver_cells, residuals, shots, doms):
    depth, width, length = forward_state.shape[2:]
    rows = velocity.shape[1]
    nrec = receiver_cells.shape[1]
    chunk = 32
    zs = shots // 4
    f32 = jnp.float32
    slab = pltpu.VMEM((depth, width, length), f32)
    wide = pltpu.VMEM((depth, width + 2 * PAD, length), f32)
    tall = pltpu.VMEM((depth + 4, width, length), f32)
    block = (2, depth, rows, length)
    dma = pltpu.SemaphoreType.DMA
    scratch = (
        [wide] * 2 + [tall] * 2 + [wide] * 2 + [tall] * 2 + [slab] * 6
        + [slab] * 4 + [slab] * 2 + [slab] * 2
        + [pltpu.VMEM((STEPS, depth, width, length), f32),
           pltpu.VMEM((depth * width, nrec), jnp.bfloat16)]
        + [pltpu.VMEM((shots,) + block, f32), pltpu.VMEM((shots,) + block, f32),
           pltpu.VMEM((2 * zs,) + block, f32), pltpu.VMEM((zs,) + block, f32),
           pltpu.VMEM((zs,) + block, f32)]
        + [dma((8,)), dma((2,)), dma((zs,)), dma((zs,)), dma((2 * zs,)), dma((shots,)),
           dma((2 * STEPS, 2)), dma((2 * STEPS, 2)),
           dma((2 * zs,)), dma((2 * zs,)), dma((zs,)), dma((zs,)), dma((zs,)), dma((zs,))]
    )
    vmem = pl.BlockSpec(memory_space=pltpu.VMEM)
    smem = pl.BlockSpec(memory_space=pltpu.SMEM)
    hbm = pl.BlockSpec(memory_space=pl.ANY)
    part = jax.ShapeDtypeStruct((depth, rows, length), f32)
    return pl.pallas_call(
        functools.partial(kernel, shots, doms, chunk),
        out_shape=(part, part),
        in_specs=[hbm, hbm, hbm, hbm, smem, smem, vmem, vmem],
        out_specs=(vmem, vmem),
        scratch_shapes=scratch,
        compiler_params=pltpu.CompilerParams(
            collective_id=0, has_side_effects=True, vmem_limit_bytes=56 * 2**20),
        name="vti_window",
    )(velocity, epsilon, forward_state, adjoint_state, source_cell, wavelet,
      receiver_cells, residuals)


def solution(mesh):
    placed = (
        P("dom", "shot", None),
        P("dom", "shot", None),
        P("shot", None, "dom", None, None),
        P("shot", None, "dom", None, None),
        P("shot"),
        P("shot", None),
        P("shot", None),
        P("shot", None, None),
    )
    return jax.shard_map(
        functools.partial(on_device, shots=mesh.shape["shot"], doms=mesh.shape["dom"]),
        mesh=mesh,
        in_specs=placed,
        out_specs=(P("dom", "shot", None), P("dom", "shot", None)),
        check_vma=False,
    )
```

```python
import functools

import jax
import jax.numpy as jnp
from jax import lax
from jax.experimental import pallas as pl
from jax.experimental.pallas import tpu as pltpu
from jax.sharding import PartitionSpec as P

STEPS = 4
PAD = 8
LANES = 128
C1, C2 = 4.0 / 3.0, 1.0 / 12.0
MESH = pl.DeviceIdType.MESH


def kernel(
    shots, doms, chunk,
    vel, eps, fwd, adj, src, wav, rec, res, out_vel, out_eps,
    p0, p1, q0, q1, w0, w1, s0, s1, a0, a1, a2, b0, b1, b2,
    flat0, flat1, dep0, dep1, img1, img2, stiff, stretch, inj, hot,
    gath, term, from_core, from_x, from_z,
    load_sem, own_sem, z_send, x_send, c_send, g_recv,
    halo_send, halo_recv, rc_send, rc_recv, rx_send, rx_recv, rz_send, rz_recv,
):
    depth, width, length = stiff.shape
    rows = vel.shape[1]
    nrec = rec.shape[1]
    zs = shots // 4
    me = lax.axis_index("shot")
    dom = lax.axis_index("dom")
    core = lax.rem(me, 2)
    xi = lax.rem(me // 2, 2)
    zi = me // 4
    n_chunks = width // chunk
    n_pairs = depth // 2
    near = 1 if doms == 2 else 2
    groups = ((0, near), (near, n_pairs))

    def shot_at(z, x, c):
        return (z * 2 + x) * 2 + c

    has_low = dom > 0
    has_high = dom < doms - 1

    def first_layer_of(place):
        if doms == 2:
            return 2 * jnp.where(has_low, place, n_pairs - 1 - place)
        end = jnp.where(place == 1, n_pairs - 1, place - 1)
        return 2 * jnp.where(place == 0, 0, end)

    loads = []

    def load(source, target):
        copy = pltpu.make_async_copy(source, target, load_sem.at[len(loads)])
        copy.start()
        loads.append(copy)

    own = []
    for place in range(n_pairs):
        pair = pl.ds(first_layer_of(place), 2)
        for i, model in enumerate((vel, eps)):
            copy = pltpu.make_async_copy(
                model.at[pair], gath.at[me, place, i], own_sem.at[place, i])
            copy.start()
            own.append(copy)
    inner = pl.ds(PAD, width)
    cells = pl.ds(2, depth)
    load(adj.at[0, 1], a1)
    load(adj.at[0, 3], b1)
    load(fwd.at[0, 1], p1.at[:, inner, :])
    load(fwd.at[0, 3], q1.at[cells])
    load(fwd.at[0, 0], p0.at[:, inner, :])
    load(fwd.at[0, 2], q0.at[cells])
    load(adj.at[0, 0], a0)
    load(adj.at[0, 2], b0)

    barrier = pltpu.get_barrier_semaphore()
    for d in range(1, zs):
        pl.semaphore_signal(
            barrier, inc=1, device_id={"shot": shot_at(lax.rem(zi + d, zs), xi, core)},
            device_id_type=MESH)
    pl.semaphore_signal(
        barrier, inc=1, device_id={"shot": shot_at(zi, 1 - xi, core)}, device_id_type=MESH)
    pl.semaphore_signal(
        barrier, inc=1, device_id={"shot": shot_at(zi, xi, 1 - core)}, device_id_type=MESH)

    @pl.when(has_low)
    def _():
        pl.semaphore_signal(barrier, inc=1, device_id={"dom": dom - 1}, device_id_type=MESH)

    @pl.when(has_high)
    def _():
        pl.semaphore_signal(barrier, inc=1, device_id={"dom": dom + 1}, device_id_type=MESH)

    beside = jnp.where(has_low, 1, 0) + jnp.where(has_high, 1, 0)
    pl.semaphore_wait(barrier, zs + 1 + beside)

    def low_copy(source, field, slot):
        return pltpu.make_async_remote_copy(
            src_ref=source, dst_ref=field.at[pl.ds(depth + 2, 2)],
            send_sem=halo_send.at[slot, 0], recv_sem=halo_recv.at[slot, 1],
            device_id={"dom": dom - 1}, device_id_type=MESH)

    def high_copy(source, field, slot):
        return pltpu.make_async_remote_copy(
            src_ref=source, dst_ref=field.at[pl.ds(0, 2)],
            send_sem=halo_send.at[slot, 1], recv_sem=halo_recv.at[slot, 0],
            device_id={"dom": dom + 1}, device_id_type=MESH)

    def send_halo(field, slot, low=None, high=None):
        low = field.at[pl.ds(2, 2)] if low is None else low
        high = field.at[pl.ds(depth, 2)] if high is None else high

        @pl.when(has_low)
        def _():
            low_copy(low, field, slot).start()

        @pl.when(has_high)
        def _():
            high_copy(high, field, slot).start()

    def wait_halo(field, slot):
        @pl.when(has_low)
        def _():
            low_copy(field.at[pl.ds(2, 2)], field, slot).wait_send()
            high_copy(field.at[pl.ds(depth, 2)], field, slot).wait_recv()

        @pl.when(has_high)
        def _():
            high_copy(field.at[pl.ds(depth, 2)], field, slot).wait_send()
            low_copy(field.at[pl.ds(2, 2)], field, slot).wait_recv()

    send_halo(q1, 0, fwd.at[0, 3, pl.ds(0, 2)], fwd.at[0, 3, pl.ds(depth - 2, 2)])

    def block_copy(g, owner, target, send_sem):
        low, high = groups[g]
        part = gath.at[owner, pl.ds(low, high - low)]
        return pltpu.make_async_remote_copy(
            src_ref=part, dst_ref=part, send_sem=send_sem, recv_sem=g_recv.at[g, owner],
            device_id={"shot": target}, device_id_type=MESH)

    def to_x(g, z):
        return block_copy(
            g, shot_at(z, xi, core), shot_at(zi, 1 - xi, core), x_send.at[g, z])

    def to_core(g, z, x):
        return block_copy(
            g, shot_at(z, x, core), shot_at(zi, xi, 1 - core), c_send.at[g, z * 2 + x])

    def to_z(g, d):
        return block_copy(
            g, me, shot_at(lax.rem(zi + d, zs), xi, core), z_send.at[g, d])

    def arrived(g, owner):
        block_copy(g, owner, me, x_send.at[g, 0]).wait_recv()

    def from_z_side(g, d):
        other = lax.rem(zi + (zs - d), zs)
        arrived(g, shot_at(other, xi, core))
        to_x(g, other).start()
        to_core(g, other, xi).start()

    def from_x_side(g, d):
        other = lax.rem(zi + (zs - d), zs)
        arrived(g, shot_at(other, 1 - xi, core))
        to_core(g, other, 1 - xi).start()

    def finish_gather(g):
        for z in range(zs):
            for x in range(2):
                arrived(g, shot_at(z, x, 1 - core))
        for d in range(1, zs):
            to_z(g, d).wait_send()
        for z in range(zs):
            to_x(g, z).wait_send()
            for x in range(2):
                to_core(g, z, x).wait_send()

        def spread(place, carry):
            pair = pl.ds(first_layer_of(place), 2)
            for s in range(shots):
                part = slice(s * rows, (s + 1) * rows)
                speed = gath[s, place, 0]
                stiff[pair, part, :] = speed * speed
                stretch[pair, part, :] = 1.0 + 2.0 * gath[s, place, 1]
            return carry

        lax.fori_loop(*groups[g], spread, 0)

    for copy in own:
        copy.wait()
    for g in range(2):
        to_x(g, zi).start()
        for d in range(1, zs):
            to_z(g, d).start()
        to_core(g, zi, xi).start()

    edge = jnp.zeros((depth, PAD, length), jnp.float32)
    for field in (p0, p1, w0, w1):
        field[:, 0:PAD, :] = edge
        field[:, PAD + width:PAD + width + PAD, :] = edge
    halo = jnp.zeros((2, width, length), jnp.float32)

    @pl.when(dom == 0)
    def _():
        for field in (q0, q1, s0, s1):
            field[0:2] = halo

    @pl.when(dom == doms - 1)
    def _():
        for field in (q0, q1, s0, s1):
            field[depth + 2:depth + 4] = halo

    first_row = dom * (depth * width)
    rec_row = rec[...] // length - first_row
    rec_col = lax.rem(rec[...], length)
    all_rows = depth * width

    def fill_hot(z, carry):
        ids = lax.broadcasted_iota(jnp.int32, (width, nrec), 0) + z * width
        hot[pl.ds(pl.multiple_of(z * width, width), width), :] = jnp.where(
            ids == rec_row, 1.0, 0.0).astype(jnp.bfloat16)
        return carry

    def inject_moment(k):
        col_hit = lax.broadcasted_iota(jnp.int32, (length, nrec), 0) == rec_col
        amount = res[0, k:k + 1, :]
        parts = []
        for _ in range(3):
            part = amount.astype(jnp.bfloat16).astype(jnp.float32)
            parts.append(jnp.where(col_hit, part, 0.0).astype(jnp.bfloat16))
            amount = amount - part

        def fill(z, carry):
            here = hot[pl.ds(pl.multiple_of(z * width, width), width), :]
            total = None
            for part in parts:
                product = lax.dot_general(
                    here, part, (((1,), (1,)), ((), ())),
                    preferred_element_type=jnp.float32)
                total = product if total is None else total + product
            inj[k, z] = total
            return carry

        lax.fori_loop(0, depth, fill, 0)

    lax.fori_loop(0, depth, fill_hot, 0)
    inject_moment(STEPS - 1)
    for d in range(1, zs):
        from_z_side(0, d)
    for d in range(zs):
        from_x_side(0, d)
    for copy in loads:
        copy.wait()
    finish_gather(0)

    lane = lax.broadcasted_iota(jnp.int32, (chunk, LANES), 1)

    def along_y(field):
        tiles = [field[:, t:t + LANES] for t in range(0, length, LANES)]

        def shifted(amount):
            turned = [pltpu.roll(t, amount % LANES, 1) for t in tiles]
            result = []
            for i in range(len(tiles)):
                if amount > 0:
                    fill = turned[i - 1] if i > 0 else 0.0
                    result.append(jnp.where(lane >= amount, turned[i], fill))
                else:
                    fill = turned[i + 1] if i + 1 < len(tiles) else 0.0
                    result.append(jnp.where(lane < LANES + amount, turned[i], fill))
            return jnp.concatenate(result, axis=1)

        return shifted(1) + shifted(-1), shifted(2) + shifted(-2)

    def lateral(field, z, r0):
        window = field[z, pl.ds(r0, chunk + 2 * PAD), :]

        def at(offset):
            turned = pltpu.roll(window, -offset % (chunk + 2 * PAD), 0)
            return turned[PAD:PAD + chunk]

        centre = window[PAD:PAD + chunk]
        near, far = along_y(centre)
        near = near + (at(1) + at(-1))
        far = far + (at(2) + at(-2))
        return centre, C1 * near - C2 * far - 5.0 * centre

    def vertical(field, z, r0):
        def at(offset):
            return field[z + (2 + offset), pl.ds(r0, chunk), :]

        centre = at(0)
        return centre, C1 * (at(1) + at(-1)) - C2 * (at(2) + at(-2)) - 2.5 * centre

    source_row = src[0] // length - first_row
    source_col = lax.rem(src[0], length)
    row_ids = lax.broadcasted_iota(jnp.int32, (chunk, length), 0)
    col_ids = lax.broadcasted_iota(jnp.int32, (chunk, length), 1)
    P_, Q_ = (p0, p1), (q0, q1)
    W_, S_ = (w0, w1), (s0, s1)

    def forward(k, z, r0, place=None, sub=None):
        now, old = (k + 1) % 2, k % 2
        here = (z, pl.ds(r0, chunk), slice(None))
        p_now, flat = lateral(P_[now], z, r0)
        q_now, dep = vertical(Q_[now], z, r0)
        if k + 1 < STEPS:
            st, sr = stiff[here], stretch[here]
            hit = (row_ids == source_row - (z * width + r0)) & (col_ids == source_col)
            pulse = jnp.where(hit, wav[0, k], 0.0)
            inside = (z, pl.ds(r0 + PAD, chunk), slice(None))
            layer = (z + 2, pl.ds(r0, chunk), slice(None))
            P_[old][inside] = 2.0 * p_now - P_[old][inside] + st * (sr * flat + dep) + pulse
            Q_[old][layer] = 2.0 * q_now - Q_[old][layer] + st * (flat + dep) + pulse
        if k == 0:
            flat0[here], dep0[here] = flat, dep
        elif k == 1:
            flat1[here], dep1[here] = flat, dep
        elif k == 2:
            a, b = a1[here], b1[here]
            img1[here] = a * flat
            img2[here] = a * dep + b * (flat + dep)
        else:
            a, b = a0[here], b0[here]
            img1[here] = img1[here] + a * flat
            img2[here] = img2[here] + (a * dep + b * (flat + dep))

    def weigh(slot, z, r0, a, b):
        here = (z, pl.ds(r0, chunk), slice(None))
        st, sr = stiff[here], stretch[here]
        W_[slot][z, pl.ds(r0 + PAD, chunk), :] = st * (sr * a + b)
        S_[slot][z + 2, pl.ds(r0, chunk), :] = st * (a + b)

    def start_adjoint(z, r0, place=None, sub=None):
        here = (z, pl.ds(r0, chunk), slice(None))
        weigh(0, z, r0, a1[here], b1[here])

    def adjoint(k, z, r0, place=None, sub=None):
        turn = STEPS - 1 - k
        old_a, now_a, new_a = ((a0, a1, a0), (a1, a0, a1), (a0, a1, a2), (a1, a2, None))[turn]
        old_b, now_b, new_b = ((b0, b1, b0), (b1, b0, b1), (b0, b1, b2), (b1, b2, None))[turn]
        here = (z, pl.ds(r0, chunk), slice(None))
        a = 2.0 * now_a[here] - old_a[here] + lateral(W_[turn % 2], z, r0)[1] + inj[(k,) + here]
        b = 2.0 * now_b[here] - old_b[here] + vertical(S_[turn % 2], z, r0)[1]
        if new_a is not None:
            new_a[here], new_b[here] = a, b
            weigh((turn + 1) % 2, z, r0, a, b)
        if k == 1:
            flat, dep = flat1[here], dep1[here]
            img1[here] = img1[here] + a * flat
            img2[here] = img2[here] + (a * dep + b * (flat + dep))
        elif k == 0:
            flat, dep = flat0[here], dep0[here]
            one = img1[here] + a * flat
            two = img2[here] + (a * dep + b * (flat + dep))
            st, sr = stiff[here], stretch[here]
            for i in range(chunk // rows):
                part = slice(i * rows, (i + 1) * rows)
                d = r0 // rows + i
                speed = gath[d, place, 0, sub]
                term[d, place, 0, sub] = 2.0 * speed * (sr[part] * one[part] + two[part])
                term[d, place, 1, sub] = 2.0 * st[part] * one[part]

    def sweep(body, g):
        low, high = groups[g]

        def turn(i, carry):
            j = i // n_chunks
            place, sub = low + j // 2, lax.rem(j, 2)
            r0 = pl.multiple_of(lax.rem(i, n_chunks) * chunk, chunk)
            body(first_layer_of(place) + sub, r0, place, sub)
            return carry

        lax.fori_loop(0, (high - low) * 2 * n_chunks, turn, 0)

    sweep(start_adjoint, 0)
    send_halo(s0, 4)
    if zs > 1:
        from_z_side(1, 1)
    wait_halo(q1, 0)
    sweep(functools.partial(forward, 0), 0)
    send_halo(q0, 1)
    for d in range(2, zs):
        from_z_side(1, d)
    inject_moment(2)
    inject_moment(1)
    for d in range(zs):
        from_x_side(1, d)
    inject_moment(0)
    finish_gather(1)
    sweep(start_adjoint, 1)
    sweep(functools.partial(forward, 0), 1)
    for turn in range(STEPS - 1):
        k = STEPS - 1 - turn
        wait_halo(S_[turn % 2], 4 + turn)
        sweep(functools.partial(adjoint, k), 0)
        send_halo(S_[(turn + 1) % 2], 5 + turn)
        sweep(functools.partial(adjoint, k), 1)
        f = turn + 1
        if f + 1 < STEPS:
            wait_halo(Q_[(f + 1) % 2], f)
            sweep(functools.partial(forward, f), 0)
            send_halo(Q_[f % 2], f + 1)
            sweep(functools.partial(forward, f), 1)

    def sum_copy(g, owner, target, index, landing, send_sem, recv_sem):
        low, high = groups[g]
        places = pl.ds(low, high - low)
        return pltpu.make_async_remote_copy(
            src_ref=term.at[owner, places], dst_ref=landing.at[index, places],
            send_sem=send_sem.at[g, index], recv_sem=recv_sem.at[g, index],
            device_id={"shot": target}, device_id_type=MESH)

    def core_sum(g, j):
        return sum_copy(
            g, 2 * j + (1 - core), shot_at(zi, xi, 1 - core), j, from_core, rc_send, rc_recv)

    def x_sum(g, z):
        return sum_copy(
            g, shot_at(z, 1 - xi, core), shot_at(zi, 1 - xi, core), z, from_x,
            rx_send, rx_recv)

    def z_sum(g, d):
        owner = shot_at(lax.rem(zi + d, zs), xi, core)
        return sum_copy(g, owner, owner, d, from_z, rz_send, rz_recv)

    pairs = chunk // rows // 2

    def last(g):
        low, high = groups[g]

        def stripe(c, carry):
            r0 = pl.multiple_of(c * chunk, chunk)

            def layer(i, inner_carry):
                place, sub = low + i // 2, lax.rem(i, 2)
                adjoint(0, first_layer_of(place) + sub, r0, place, sub)
                return inner_carry

            lax.fori_loop(0, (high - low) * 2, layer, 0)
            for i in range(pairs):
                core_sum(g, c * pairs + i).start()
            return carry

        lax.fori_loop(0, n_chunks, stripe, 0)

    def add(g, owner, landing, index):
        low, high = groups[g]
        places = pl.ds(low, high - low)
        term[owner, places] = term[owner, places] + landing[index, places]

    order = list(range(1, zs)) + [0]

    def sum_cores(g):
        for x, side in ((1 - xi, True), (xi, False)):
            for d in order:
                z = lax.rem(zi + d, zs)
                j = z * 2 + x
                core_sum(g, j).wait_recv()
                add(g, 2 * j + core, from_core, j)
                if side:
                    x_sum(g, z).start()

    def sum_x(g):
        for d in order:
            z = lax.rem(zi + d, zs)
            x_sum(g, z).wait_recv()
            add(g, shot_at(z, xi, core), from_x, z)
            if d > 0:
                z_sum(g, d).start()

    def sum_z(g):
        low, high = groups[g]
        for d in range(1, zs):
            z_sum(g, d).wait_recv()
        for place in range(low, high):
            total = term[me, place]
            for d in range(1, zs):
                total = total + from_z[d, place]
            pair = pl.ds(first_layer_of(place), 2)
            out_vel[pair] = total[0]
            out_eps[pair] = total[1]

    sweep(functools.partial(forward, STEPS - 1), 1)
    last(1)
    sum_cores(1)
    wait_halo(Q_[STEPS % 2], STEPS - 1)
    sweep(functools.partial(forward, STEPS - 1), 0)
    wait_halo(S_[(STEPS - 1) % 2], 3 + STEPS)
    last(0)
    sum_x(1)
    sum_cores(0)
    sum_x(0)
    sum_z(1)
    sum_z(0)
    for g in range(2):
        for j in range(2 * zs):
            core_sum(g, j).wait_send()
        for z in range(zs):
            x_sum(g, z).wait_send()
        for d in range(1, zs):
            z_sum(g, d).wait_send()


def on_device(velocity, epsilon, forward_state, adjoint_state, source_cell, wavelet,
              receiver_cells, residuals, shots, doms):
    depth, width, length = forward_state.shape[2:]
    rows = velocity.shape[1]
    nrec = receiver_cells.shape[1]
    chunk = 32
    zs = shots // 4
    f32 = jnp.float32
    slab = pltpu.VMEM((depth, width, length), f32)
    wide = pltpu.VMEM((depth, width + 2 * PAD, length), f32)
    tall = pltpu.VMEM((depth + 4, width, length), f32)
    block = (depth // 2, 2, 2, rows, length)
    dma = pltpu.SemaphoreType.DMA
    scratch = (
        [wide] * 2 + [tall] * 2 + [wide] * 2 + [tall] * 2 + [slab] * 6
        + [slab] * 4 + [slab] * 2 + [slab] * 2
        + [pltpu.VMEM((STEPS, depth, width, length), f32),
           pltpu.VMEM((depth * width, nrec), jnp.bfloat16)]
        + [pltpu.VMEM((shots,) + block, f32), pltpu.VMEM((shots,) + block, f32),
           pltpu.VMEM((2 * zs,) + block, f32), pltpu.VMEM((zs,) + block, f32),
           pltpu.VMEM((zs,) + block, f32)]
        + [dma((8,)), dma((depth // 2, 2)),
           dma((2, zs)), dma((2, zs)), dma((2, 2 * zs)), dma((2, shots)),
           dma((2 * STEPS, 2)), dma((2 * STEPS, 2)),
           dma((2, 2 * zs)), dma((2, 2 * zs)), dma((2, zs)), dma((2, zs)),
           dma((2, zs)), dma((2, zs))]
    )
    vmem = pl.BlockSpec(memory_space=pltpu.VMEM)
    smem = pl.BlockSpec(memory_space=pltpu.SMEM)
    hbm = pl.BlockSpec(memory_space=pl.ANY)
    part = jax.ShapeDtypeStruct((depth, rows, length), f32)
    return pl.pallas_call(
        functools.partial(kernel, shots, doms, chunk),
        out_shape=(part, part),
        in_specs=[hbm, hbm, hbm, hbm, smem, smem, vmem, vmem],
        out_specs=(vmem, vmem),
        scratch_shapes=scratch,
        compiler_params=pltpu.CompilerParams(
            collective_id=0, has_side_effects=True, vmem_limit_bytes=56 * 2**20),
        name="vti_window",
    )(velocity, epsilon, forward_state, adjoint_state, source_cell, wavelet,
      receiver_cells, residuals)


def solution(mesh):
    placed = (
        P("dom", "shot", None),
        P("dom", "shot", None),
        P("shot", None, "dom", None, None),
        P("shot", None, "dom", None, None),
        P("shot"),
        P("shot", None),
        P("shot", None),
        P("shot", None, None),
    )
    return jax.shard_map(
        functools.partial(on_device, shots=mesh.shape["shot"], doms=mesh.shape["dom"]),
        mesh=mesh,
        in_specs=placed,
        out_specs=(P("dom", "shot", None), P("dom", "shot", None)),
        check_vma=False,
    )
```

```python
import functools

import jax
import jax.numpy as jnp
from jax import lax
from jax.experimental import pallas as pl
from jax.experimental.pallas import tpu as pltpu
from jax.sharding import PartitionSpec as P

STEPS = 4
PAD = 8
LANES = 128
C1, C2 = 4.0 / 3.0, 1.0 / 12.0
MESH = pl.DeviceIdType.MESH


def kernel(
    shots, doms, chunk,
    vel, eps, fwd, adj, src, wav, rec, res, out_vel, out_eps,
    p0, p1, q0, q1, w0, w1, s0, s1, a0, a1, a2, b0, b1, b2,
    flat0, flat1, dep0, dep1, img1, img2, stiff, stretch, inj, hot,
    gath, term, from_core, from_x, from_z,
    load_sem, own_sem, z_send, x_send, c_send, g_recv,
    halo_send, halo_recv, rc_send, rc_recv, rx_send, rx_recv, rz_send, rz_recv,
):
    depth, width, length = stiff.shape
    rows = vel.shape[1]
    nrec = rec.shape[1]
    zs = shots // 4
    me = lax.axis_index("shot")
    dom = lax.axis_index("dom")
    core = lax.rem(me, 2)
    xi = lax.rem(me // 2, 2)
    zi = me // 4
    n_chunks = width // chunk
    n_pairs = depth // 2
    near = 1 if doms == 2 else 2
    groups = ((0, near), (near, n_pairs))

    def shot_at(z, x, c):
        return (z * 2 + x) * 2 + c

    has_low = dom > 0
    has_high = dom < doms - 1

    def first_layer_of(place):
        if doms == 2:
            return 2 * jnp.where(has_low, place, n_pairs - 1 - place)
        end = jnp.where(place == 1, n_pairs - 1, place - 1)
        return 2 * jnp.where(place == 0, 0, end)

    loads = []

    def load(source, target):
        copy = pltpu.make_async_copy(source, target, load_sem.at[len(loads)])
        copy.start()
        loads.append(copy)

    own = []
    for place in range(n_pairs):
        pair = pl.ds(first_layer_of(place), 2)
        for i, model in enumerate((vel, eps)):
            copy = pltpu.make_async_copy(
                model.at[pair], gath.at[me, place, i], own_sem.at[place, i])
            copy.start()
            own.append(copy)
    inner = pl.ds(PAD, width)
    cells = pl.ds(2, depth)
    load(adj.at[0, 1], a1)
    load(adj.at[0, 3], b1)
    tiles = length // LANES
    for t in range(tiles):
        load(fwd.at[0, 1, :, :, pl.ds(t * LANES, LANES)], p1.at[:, t, inner, :])
    load(fwd.at[0, 3], q1.at[cells])
    for t in range(tiles):
        load(fwd.at[0, 0, :, :, pl.ds(t * LANES, LANES)], p0.at[:, t, inner, :])
    load(fwd.at[0, 2], q0.at[cells])
    load(adj.at[0, 0], a0)
    load(adj.at[0, 2], b0)

    barrier = pltpu.get_barrier_semaphore()
    for d in range(1, zs):
        pl.semaphore_signal(
            barrier, inc=1, device_id={"shot": shot_at(lax.rem(zi + d, zs), xi, core)},
            device_id_type=MESH)
    pl.semaphore_signal(
        barrier, inc=1, device_id={"shot": shot_at(zi, 1 - xi, core)}, device_id_type=MESH)
    pl.semaphore_signal(
        barrier, inc=1, device_id={"shot": shot_at(zi, xi, 1 - core)}, device_id_type=MESH)

    @pl.when(has_low)
    def _():
        pl.semaphore_signal(barrier, inc=1, device_id={"dom": dom - 1}, device_id_type=MESH)

    @pl.when(has_high)
    def _():
        pl.semaphore_signal(barrier, inc=1, device_id={"dom": dom + 1}, device_id_type=MESH)

    beside = jnp.where(has_low, 1, 0) + jnp.where(has_high, 1, 0)
    pl.semaphore_wait(barrier, zs + 1 + beside)

    def low_copy(source, field, slot):
        return pltpu.make_async_remote_copy(
            src_ref=source, dst_ref=field.at[pl.ds(depth + 2, 2)],
            send_sem=halo_send.at[slot, 0], recv_sem=halo_recv.at[slot, 1],
            device_id={"dom": dom - 1}, device_id_type=MESH)

    def high_copy(source, field, slot):
        return pltpu.make_async_remote_copy(
            src_ref=source, dst_ref=field.at[pl.ds(0, 2)],
            send_sem=halo_send.at[slot, 1], recv_sem=halo_recv.at[slot, 0],
            device_id={"dom": dom + 1}, device_id_type=MESH)

    def send_halo(field, slot, low=None, high=None):
        low = field.at[pl.ds(2, 2)] if low is None else low
        high = field.at[pl.ds(depth, 2)] if high is None else high

        @pl.when(has_low)
        def _():
            low_copy(low, field, slot).start()

        @pl.when(has_high)
        def _():
            high_copy(high, field, slot).start()

    def wait_halo(field, slot):
        @pl.when(has_low)
        def _():
            low_copy(field.at[pl.ds(2, 2)], field, slot).wait_send()
            high_copy(field.at[pl.ds(depth, 2)], field, slot).wait_recv()

        @pl.when(has_high)
        def _():
            high_copy(field.at[pl.ds(depth, 2)], field, slot).wait_send()
            low_copy(field.at[pl.ds(2, 2)], field, slot).wait_recv()

    send_halo(q1, 0, fwd.at[0, 3, pl.ds(0, 2)], fwd.at[0, 3, pl.ds(depth - 2, 2)])

    def block_copy(g, owner, target, send_sem):
        low, high = groups[g]
        part = gath.at[owner, pl.ds(low, high - low)]
        return pltpu.make_async_remote_copy(
            src_ref=part, dst_ref=part, send_sem=send_sem, recv_sem=g_recv.at[g, owner],
            device_id={"shot": target}, device_id_type=MESH)

    def to_x(g, z):
        return block_copy(
            g, shot_at(z, xi, core), shot_at(zi, 1 - xi, core), x_send.at[g, z])

    def to_core(g, z, x):
        return block_copy(
            g, shot_at(z, x, core), shot_at(zi, xi, 1 - core), c_send.at[g, z * 2 + x])

    def to_z(g, d):
        return block_copy(
            g, me, shot_at(lax.rem(zi + d, zs), xi, core), z_send.at[g, d])

    def arrived(g, owner):
        block_copy(g, owner, me, x_send.at[g, 0]).wait_recv()

    def from_z_side(g, d):
        other = lax.rem(zi + (zs - d), zs)
        arrived(g, shot_at(other, xi, core))
        to_x(g, other).start()
        to_core(g, other, xi).start()

    def from_x_side(g, d):
        other = lax.rem(zi + (zs - d), zs)
        arrived(g, shot_at(other, 1 - xi, core))
        to_core(g, other, 1 - xi).start()

    def finish_gather(g):
        for z in range(zs):
            for x in range(2):
                arrived(g, shot_at(z, x, 1 - core))
        for d in range(1, zs):
            to_z(g, d).wait_send()
        for z in range(zs):
            to_x(g, z).wait_send()
            for x in range(2):
                to_core(g, z, x).wait_send()

        def spread(place, carry):
            pair = pl.ds(first_layer_of(place), 2)
            for s in range(shots):
                part = slice(s * rows, (s + 1) * rows)
                speed = gath[s, place, 0]
                stiff[pair, part, :] = speed * speed
                stretch[pair, part, :] = 1.0 + 2.0 * gath[s, place, 1]
            return carry

        lax.fori_loop(*groups[g], spread, 0)

    for copy in own:
        copy.wait()
    for g in range(2):
        to_x(g, zi).start()
        for d in range(1, zs):
            to_z(g, d).start()
        to_core(g, zi, xi).start()

    edge = jnp.zeros((depth, tiles, PAD, LANES), jnp.float32)
    for field in (p0, p1, w0, w1):
        field[:, :, 0:PAD, :] = edge
        field[:, :, PAD + width:PAD + width + PAD, :] = edge
    halo = jnp.zeros((2, width, length), jnp.float32)

    @pl.when(dom == 0)
    def _():
        for field in (q0, q1, s0, s1):
            field[0:2] = halo

    @pl.when(dom == doms - 1)
    def _():
        for field in (q0, q1, s0, s1):
            field[depth + 2:depth + 4] = halo

    first_row = dom * (depth * width)
    rec_row = rec[...] // length - first_row
    rec_col = lax.rem(rec[...], length)
    all_rows = depth * width

    def fill_hot(z, carry):
        ids = lax.broadcasted_iota(jnp.int32, (width, nrec), 0) + z * width
        hot[pl.ds(pl.multiple_of(z * width, width), width), :] = jnp.where(
            ids == rec_row, 1.0, 0.0).astype(jnp.bfloat16)
        return carry

    def inject_moment(k):
        col_hit = lax.broadcasted_iota(jnp.int32, (length, nrec), 0) == rec_col
        amount = res[0, k:k + 1, :]
        parts = []
        for _ in range(3):
            part = amount.astype(jnp.bfloat16).astype(jnp.float32)
            parts.append(jnp.where(col_hit, part, 0.0).astype(jnp.bfloat16))
            amount = amount - part

        def fill(z, carry):
            here = hot[pl.ds(pl.multiple_of(z * width, width), width), :]
            total = None
            for part in parts:
                product = lax.dot_general(
                    here, part, (((1,), (1,)), ((), ())),
                    preferred_element_type=jnp.float32)
                total = product if total is None else total + product
            inj[k, z] = total
            return carry

        lax.fori_loop(0, depth, fill, 0)

    lax.fori_loop(0, depth, fill_hot, 0)
    inject_moment(STEPS - 1)
    for d in range(1, zs):
        from_z_side(0, d)
    for d in range(zs):
        from_x_side(0, d)
    for copy in loads:
        copy.wait()
    finish_gather(0)

    lane = lax.broadcasted_iota(jnp.int32, (chunk, LANES), 1)

    def lateral(field, z, r0):
        def at(t, offset):
            return field[z, t, pl.ds(r0 + (PAD + offset), chunk), :]

        centre = [at(t, 0) for t in range(tiles)]

        def shifted(amount):
            turned = [pltpu.roll(t, amount % LANES, 1) for t in centre]
            result = []
            for i in range(tiles):
                if amount > 0:
                    fill = turned[i - 1] if i > 0 else 0.0
                    result.append(jnp.where(lane >= amount, turned[i], fill))
                else:
                    fill = turned[i + 1] if i + 1 < tiles else 0.0
                    result.append(jnp.where(lane < LANES + amount, turned[i], fill))
            return result

        up1, down1, up2, down2 = shifted(1), shifted(-1), shifted(2), shifted(-2)
        result = []
        for t in range(tiles):
            close = (up1[t] + down1[t]) + (at(t, 1) + at(t, -1))
            remote = (up2[t] + down2[t]) + (at(t, 2) + at(t, -2))
            result.append(C1 * close - C2 * remote - 5.0 * centre[t])
        return jnp.concatenate(centre, axis=1), jnp.concatenate(result, axis=1)

    def get_tiles(field, z, r0):
        return jnp.concatenate(
            [field[z, t, pl.ds(r0 + PAD, chunk), :] for t in range(tiles)], axis=1)

    def put_tiles(field, z, r0, value):
        for t in range(tiles):
            field[z, t, pl.ds(r0 + PAD, chunk), :] = value[:, t * LANES:(t + 1) * LANES]

    def vertical(field, z, r0):
        def at(offset):
            return field[z + (2 + offset), pl.ds(r0, chunk), :]

        centre = at(0)
        return centre, C1 * (at(1) + at(-1)) - C2 * (at(2) + at(-2)) - 2.5 * centre

    source_row = src[0] // length - first_row
    source_col = lax.rem(src[0], length)
    row_ids = lax.broadcasted_iota(jnp.int32, (chunk, length), 0)
    col_hit = lax.broadcasted_iota(jnp.int32, (1, length), 1) == source_col
    P_, Q_ = (p0, p1), (q0, q1)
    W_, S_ = (w0, w1), (s0, s1)

    def forward(k, z, r0, place=None, sub=None):
        now, old = (k + 1) % 2, k % 2
        here = (z, pl.ds(r0, chunk), slice(None))
        p_now, flat = lateral(P_[now], z, r0)
        q_now, dep = vertical(Q_[now], z, r0)
        if k + 1 < STEPS:
            st, sr = stiff[here], stretch[here]
            pulse = jnp.where(
                row_ids == source_row - (z * width + r0),
                jnp.where(col_hit, wav[0, k], 0.0), 0.0)
            layer = (z + 2, pl.ds(r0, chunk), slice(None))
            p_old, q_old = get_tiles(P_[old], z, r0), Q_[old][layer]
            p_new = 2.0 * p_now - p_old + st * (sr * flat + dep) + pulse
            q_new = 2.0 * q_now - q_old + st * (flat + dep) + pulse
            put_tiles(P_[old], z, r0, p_new)
            Q_[old][layer] = q_new
        if k == 0:
            flat0[here], dep0[here] = flat, dep
        elif k == 1:
            flat1[here], dep1[here] = flat, dep
        elif k == 2:
            a, b = a1[here], b1[here]
            img1[here] = a * flat
            img2[here] = a * dep + b * (flat + dep)
        else:
            a, b = a0[here], b0[here]
            img1[here] = img1[here] + a * flat
            img2[here] = img2[here] + (a * dep + b * (flat + dep))

    def weigh(slot, z, r0, a, b):
        here = (z, pl.ds(r0, chunk), slice(None))
        st, sr = stiff[here], stretch[here]
        put_tiles(W_[slot], z, r0, st * (sr * a + b))
        S_[slot][z + 2, pl.ds(r0, chunk), :] = st * (a + b)

    def start_adjoint(z, r0, place=None, sub=None):
        here = (z, pl.ds(r0, chunk), slice(None))
        weigh(0, z, r0, a1[here], b1[here])

    def adjoint(k, z, r0, place=None, sub=None):
        turn = STEPS - 1 - k
        old_a, now_a, new_a = ((a0, a1, a0), (a1, a0, a1), (a0, a1, a2), (a1, a2, None))[turn]
        old_b, now_b, new_b = ((b0, b1, b0), (b1, b0, b1), (b0, b1, b2), (b1, b2, None))[turn]
        here = (z, pl.ds(r0, chunk), slice(None))
        a = 2.0 * now_a[here] - old_a[here] + lateral(W_[turn % 2], z, r0)[1] + inj[(k,) + here]
        b = 2.0 * now_b[here] - old_b[here] + vertical(S_[turn % 2], z, r0)[1]
        if new_a is not None:
            new_a[here], new_b[here] = a, b
            weigh((turn + 1) % 2, z, r0, a, b)
        if k == 1:
            flat, dep = flat1[here], dep1[here]
            img1[here] = img1[here] + a * flat
            img2[here] = img2[here] + (a * dep + b * (flat + dep))
        elif k == 0:
            flat, dep = flat0[here], dep0[here]
            one = img1[here] + a * flat
            two = img2[here] + (a * dep + b * (flat + dep))
            st, sr = stiff[here], stretch[here]
            for i in range(chunk // rows):
                part = slice(i * rows, (i + 1) * rows)
                d = r0 // rows + i
                speed = gath[d, place, 0, sub]
                term[d, place, 0, sub] = 2.0 * speed * (sr[part] * one[part] + two[part])
                term[d, place, 1, sub] = 2.0 * st[part] * one[part]

    def sweep(body, g):
        low, high = groups[g]

        def turn(i, carry):
            j = i // n_chunks
            place, sub = low + j // 2, lax.rem(j, 2)
            r0 = pl.multiple_of(lax.rem(i, n_chunks) * chunk, chunk)
            body(first_layer_of(place) + sub, r0, place, sub)
            return carry

        lax.fori_loop(0, (high - low) * 2 * n_chunks, turn, 0)

    sweep(start_adjoint, 0)
    send_halo(s0, 4)
    if zs > 1:
        from_z_side(1, 1)
    wait_halo(q1, 0)
    sweep(functools.partial(forward, 0), 0)
    send_halo(q0, 1)
    for d in range(2, zs):
        from_z_side(1, d)
    inject_moment(2)
    inject_moment(1)
    for d in range(zs):
        from_x_side(1, d)
    inject_moment(0)
    finish_gather(1)
    sweep(start_adjoint, 1)
    sweep(functools.partial(forward, 0), 1)
    for turn in range(STEPS - 1):
        k = STEPS - 1 - turn
        wait_halo(S_[turn % 2], 4 + turn)
        sweep(functools.partial(adjoint, k), 0)
        send_halo(S_[(turn + 1) % 2], 5 + turn)
        sweep(functools.partial(adjoint, k), 1)
        f = turn + 1
        if f + 1 < STEPS:
            wait_halo(Q_[(f + 1) % 2], f)
            sweep(functools.partial(forward, f), 0)
            send_halo(Q_[f % 2], f + 1)
            sweep(functools.partial(forward, f), 1)

    def sum_copy(g, owner, target, index, landing, send_sem, recv_sem):
        low, high = groups[g]
        places = pl.ds(low, high - low)
        return pltpu.make_async_remote_copy(
            src_ref=term.at[owner, places], dst_ref=landing.at[index, places],
            send_sem=send_sem.at[g, index], recv_sem=recv_sem.at[g, index],
            device_id={"shot": target}, device_id_type=MESH)

    def core_sum(g, j):
        return sum_copy(
            g, 2 * j + (1 - core), shot_at(zi, xi, 1 - core), j, from_core, rc_send, rc_recv)

    def x_sum(g, z):
        return sum_copy(
            g, shot_at(z, 1 - xi, core), shot_at(zi, 1 - xi, core), z, from_x,
            rx_send, rx_recv)

    def z_sum(g, d):
        owner = shot_at(lax.rem(zi + d, zs), xi, core)
        return sum_copy(g, owner, owner, d, from_z, rz_send, rz_recv)

    pairs = chunk // rows // 2

    def last(g):
        low, high = groups[g]

        def stripe(c, carry):
            r0 = pl.multiple_of(c * chunk, chunk)

            def layer(i, inner_carry):
                place, sub = low + i // 2, lax.rem(i, 2)
                adjoint(0, first_layer_of(place) + sub, r0, place, sub)
                return inner_carry

            lax.fori_loop(0, (high - low) * 2, layer, 0)
            for i in range(pairs):
                core_sum(g, c * pairs + i).start()
            return carry

        lax.fori_loop(0, n_chunks, stripe, 0)

    def add(g, owner, landing, index):
        low, high = groups[g]
        places = pl.ds(low, high - low)
        term[owner, places] = term[owner, places] + landing[index, places]

    order = list(range(1, zs)) + [0]

    def sum_cores(g):
        for x, side in ((1 - xi, True), (xi, False)):
            for d in order:
                z = lax.rem(zi + d, zs)
                j = z * 2 + x
                core_sum(g, j).wait_recv()
                add(g, 2 * j + core, from_core, j)
                if side:
                    x_sum(g, z).start()

    def sum_x(g):
        for d in order:
            z = lax.rem(zi + d, zs)
            x_sum(g, z).wait_recv()
            add(g, shot_at(z, xi, core), from_x, z)
            if d > 0:
                z_sum(g, d).start()

    def sum_z(g):
        low, high = groups[g]
        for d in range(1, zs):
            z_sum(g, d).wait_recv()
        for place in range(low, high):
            total = term[me, place]
            for d in range(1, zs):
                total = total + from_z[d, place]
            pair = pl.ds(first_layer_of(place), 2)
            out_vel[pair] = total[0]
            out_eps[pair] = total[1]

    sweep(functools.partial(forward, STEPS - 1), 1)
    last(1)
    sum_cores(1)
    wait_halo(Q_[STEPS % 2], STEPS - 1)
    sweep(functools.partial(forward, STEPS - 1), 0)
    wait_halo(S_[(STEPS - 1) % 2], 3 + STEPS)
    last(0)
    sum_x(1)
    sum_cores(0)
    sum_x(0)
    sum_z(1)
    sum_z(0)
    for g in range(2):
        for j in range(2 * zs):
            core_sum(g, j).wait_send()
        for z in range(zs):
            x_sum(g, z).wait_send()
        for d in range(1, zs):
            z_sum(g, d).wait_send()


def on_device(velocity, epsilon, forward_state, adjoint_state, source_cell, wavelet,
              receiver_cells, residuals, shots, doms):
    depth, width, length = forward_state.shape[2:]
    rows = velocity.shape[1]
    nrec = receiver_cells.shape[1]
    chunk = 64
    zs = shots // 4
    f32 = jnp.float32
    slab = pltpu.VMEM((depth, width, length), f32)
    wide = pltpu.VMEM((depth, length // LANES, width + 2 * PAD, LANES), f32)
    tall = pltpu.VMEM((depth + 4, width, length), f32)
    block = (depth // 2, 2, 2, rows, length)
    dma = pltpu.SemaphoreType.DMA
    scratch = (
        [wide] * 2 + [tall] * 2 + [wide] * 2 + [tall] * 2 + [slab] * 6
        + [slab] * 4 + [slab] * 2 + [slab] * 2
        + [pltpu.VMEM((STEPS, depth, width, length), f32),
           pltpu.VMEM((depth * width, nrec), jnp.bfloat16)]
        + [pltpu.VMEM((shots,) + block, f32), pltpu.VMEM((shots,) + block, f32),
           pltpu.VMEM((2 * zs,) + block, f32), pltpu.VMEM((zs,) + block, f32),
           pltpu.VMEM((zs,) + block, f32)]
        + [dma((6 + 2 * (length // LANES),)), dma((depth // 2, 2)),
           dma((2, zs)), dma((2, zs)), dma((2, 2 * zs)), dma((2, shots)),
           dma((2 * STEPS, 2)), dma((2 * STEPS, 2)),
           dma((2, 2 * zs)), dma((2, 2 * zs)), dma((2, zs)), dma((2, zs)),
           dma((2, zs)), dma((2, zs))]
    )
    vmem = pl.BlockSpec(memory_space=pltpu.VMEM)
    smem = pl.BlockSpec(memory_space=pltpu.SMEM)
    hbm = pl.BlockSpec(memory_space=pl.ANY)
    part = jax.ShapeDtypeStruct((depth, rows, length), f32)
    return pl.pallas_call(
        functools.partial(kernel, shots, doms, chunk),
        out_shape=(part, part),
        in_specs=[hbm, hbm, hbm, hbm, smem, smem, vmem, vmem],
        out_specs=(vmem, vmem),
        scratch_shapes=scratch,
        compiler_params=pltpu.CompilerParams(
            collective_id=0, has_side_effects=True, vmem_limit_bytes=56 * 2**20),
        name="vti_window",
    )(velocity, epsilon, forward_state, adjoint_state, source_cell, wavelet,
      receiver_cells, residuals)


def solution(mesh):
    placed = (
        P("dom", "shot", None),
        P("dom", "shot", None),
        P("shot", None, "dom", None, None),
        P("shot", None, "dom", None, None),
        P("shot"),
        P("shot", None),
        P("shot", None),
        P("shot", None, None),
    )
    return jax.shard_map(
        functools.partial(on_device, shots=mesh.shape["shot"], doms=mesh.shape["dom"]),
        mesh=mesh,
        in_specs=placed,
        out_specs=(P("dom", "shot", None), P("dom", "shot", None)),
        check_vma=False,
    )
```

```python
import functools

import jax
import jax.numpy as jnp
from jax import lax
from jax.experimental import pallas as pl
from jax.experimental.pallas import tpu as pltpu
from jax.sharding import PartitionSpec as P

STEPS = 4
PAD = 8
LANES = 128
C1, C2 = 4.0 / 3.0, 1.0 / 12.0
MESH = pl.DeviceIdType.MESH


def kernel(
    shots, doms, chunk,
    vel, eps, fwd, adj, src, wav, rec, res, out,
    p0, p1, q0, q1, w0, w1, s0, s1, a0, a1, a2, b0, b1, b2,
    flat0, flat1, dep0, dep1, img1, img2, stiff, stretch, inj, hot,
    gath, term, from_core, from_x, from_z,
    load_sem, own_sem, z_send, x_send, c_send, g_recv,
    halo_send, halo_recv, rc_send, rc_recv, rx_send, rx_recv, rz_send, rz_recv,
):
    depth, width, length = stiff.shape
    rows = vel.shape[1]
    nrec = rec.shape[1]
    zs = shots // 4
    me = lax.axis_index("shot")
    dom = lax.axis_index("dom")
    core = lax.rem(me, 2)
    xi = lax.rem(me // 2, 2)
    zi = me // 4
    n_chunks = width // chunk
    n_pairs = depth // 2
    near = 1 if doms == 2 else 2
    groups = ((0, near), (near, n_pairs))

    def shot_at(z, x, c):
        return (z * 2 + x) * 2 + c

    has_low = dom > 0
    has_high = dom < doms - 1

    def first_layer_of(place):
        if doms == 2:
            return 2 * jnp.where(has_low, place, n_pairs - 1 - place)
        end = jnp.where(place == 1, n_pairs - 1, place - 1)
        return 2 * jnp.where(place == 0, 0, end)

    loads = []

    def load(source, target):
        copy = pltpu.make_async_copy(source, target, load_sem.at[len(loads)])
        copy.start()
        loads.append(copy)

    own = []
    for place in range(n_pairs):
        pair = pl.ds(first_layer_of(place), 2)
        for i, model in enumerate((vel, eps)):
            copy = pltpu.make_async_copy(
                model.at[pair], gath.at[me, place, i], own_sem.at[place, i])
            copy.start()
            own.append(copy)
    inner = pl.ds(PAD, width)
    cells = pl.ds(2, depth)
    load(adj.at[0, 1], a1)
    load(adj.at[0, 3], b1)
    tiles = length // LANES
    for t in range(tiles):
        load(fwd.at[0, 1, :, :, pl.ds(t * LANES, LANES)], p1.at[:, t, inner, :])
    load(fwd.at[0, 3], q1.at[cells])
    for t in range(tiles):
        load(fwd.at[0, 0, :, :, pl.ds(t * LANES, LANES)], p0.at[:, t, inner, :])
    load(fwd.at[0, 2], q0.at[cells])
    load(adj.at[0, 0], a0)
    load(adj.at[0, 2], b0)

    barrier = pltpu.get_barrier_semaphore()
    for d in range(1, zs):
        pl.semaphore_signal(
            barrier, inc=1, device_id={"shot": shot_at(lax.rem(zi + d, zs), xi, core)},
            device_id_type=MESH)
    pl.semaphore_signal(
        barrier, inc=1, device_id={"shot": shot_at(zi, 1 - xi, core)}, device_id_type=MESH)
    pl.semaphore_signal(
        barrier, inc=1, device_id={"shot": shot_at(zi, xi, 1 - core)}, device_id_type=MESH)

    @pl.when(has_low)
    def _():
        pl.semaphore_signal(barrier, inc=1, device_id={"dom": dom - 1}, device_id_type=MESH)

    @pl.when(has_high)
    def _():
        pl.semaphore_signal(barrier, inc=1, device_id={"dom": dom + 1}, device_id_type=MESH)

    beside = jnp.where(has_low, 1, 0) + jnp.where(has_high, 1, 0)
    pl.semaphore_wait(barrier, zs + 1 + beside)

    def low_copy(source, field, slot, c):
        stripe = pl.ds(pl.multiple_of(c * chunk, chunk), chunk)
        return pltpu.make_async_remote_copy(
            src_ref=source.at[:, stripe, :], dst_ref=field.at[pl.ds(depth + 2, 2), stripe, :],
            send_sem=halo_send.at[slot, 0, c], recv_sem=halo_recv.at[slot, 1, c],
            device_id={"dom": dom - 1}, device_id_type=MESH)

    def high_copy(source, field, slot, c):
        stripe = pl.ds(pl.multiple_of(c * chunk, chunk), chunk)
        return pltpu.make_async_remote_copy(
            src_ref=source.at[:, stripe, :], dst_ref=field.at[pl.ds(0, 2), stripe, :],
            send_sem=halo_send.at[slot, 1, c], recv_sem=halo_recv.at[slot, 0, c],
            device_id={"dom": dom + 1}, device_id_type=MESH)

    def send_halo(field, slot, c, low=None, high=None):
        low = field.at[pl.ds(2, 2)] if low is None else low
        high = field.at[pl.ds(depth, 2)] if high is None else high

        @pl.when(has_low)
        def _():
            low_copy(low, field, slot, c).start()

        @pl.when(has_high)
        def _():
            high_copy(high, field, slot, c).start()

    def wait_halo(field, slot, c):
        low, high = field.at[pl.ds(2, 2)], field.at[pl.ds(depth, 2)]

        @pl.when(has_low)
        def _():
            low_copy(low, field, slot, c).wait_send()
            high_copy(high, field, slot, c).wait_recv()

        @pl.when(has_high)
        def _():
            high_copy(high, field, slot, c).wait_send()
            low_copy(low, field, slot, c).wait_recv()

    for c in range(n_chunks):
        send_halo(
            q1, 0, c, fwd.at[0, 3, pl.ds(0, 2)], fwd.at[0, 3, pl.ds(depth - 2, 2)])

    def block_copy(g, owner, target, send_sem):
        low, high = groups[g]
        part = gath.at[owner, pl.ds(low, high - low)]
        return pltpu.make_async_remote_copy(
            src_ref=part, dst_ref=part, send_sem=send_sem, recv_sem=g_recv.at[g, owner],
            device_id={"shot": target}, device_id_type=MESH)

    def to_x(g, z):
        return block_copy(
            g, shot_at(z, xi, core), shot_at(zi, 1 - xi, core), x_send.at[g, z])

    def to_core(g, z, x):
        return block_copy(
            g, shot_at(z, x, core), shot_at(zi, xi, 1 - core), c_send.at[g, z * 2 + x])

    def to_z(g, d):
        return block_copy(
            g, me, shot_at(lax.rem(zi + d, zs), xi, core), z_send.at[g, d])

    def arrived(g, owner):
        block_copy(g, owner, me, x_send.at[g, 0]).wait_recv()

    def from_z_side(g, d):
        other = lax.rem(zi + (zs - d), zs)
        arrived(g, shot_at(other, xi, core))
        to_x(g, other).start()
        to_core(g, other, xi).start()

    def from_x_side(g, d):
        other = lax.rem(zi + (zs - d), zs)
        arrived(g, shot_at(other, 1 - xi, core))
        to_core(g, other, 1 - xi).start()

    def finish_gather(g):
        for z in range(zs):
            for x in range(2):
                arrived(g, shot_at(z, x, 1 - core))
        for d in range(1, zs):
            to_z(g, d).wait_send()
        for z in range(zs):
            to_x(g, z).wait_send()
            for x in range(2):
                to_core(g, z, x).wait_send()

        def spread(place, carry):
            pair = pl.ds(first_layer_of(place), 2)
            for s in range(shots):
                part = slice(s * rows, (s + 1) * rows)
                speed = gath[s, place, 0]
                stiff[pair, part, :] = speed * speed
                stretch[pair, part, :] = 1.0 + 2.0 * gath[s, place, 1]
            return carry

        lax.fori_loop(*groups[g], spread, 0)

    for copy in own:
        copy.wait()
    for g in range(2):
        to_x(g, zi).start()
        for d in range(1, zs):
            to_z(g, d).start()
        to_core(g, zi, xi).start()

    edge = jnp.zeros((depth, tiles, PAD, LANES), jnp.float32)
    for field in (p0, p1, w0, w1):
        field[:, :, 0:PAD, :] = edge
        field[:, :, PAD + width:PAD + width + PAD, :] = edge
    halo = jnp.zeros((2, width, length), jnp.float32)

    @pl.when(dom == 0)
    def _():
        for field in (q0, q1, s0, s1):
            field[0:2] = halo

    @pl.when(dom == doms - 1)
    def _():
        for field in (q0, q1, s0, s1):
            field[depth + 2:depth + 4] = halo

    first_row = dom * (depth * width)
    rec_row = rec[...] // length - first_row
    rec_col = lax.rem(rec[...], length)
    all_rows = depth * width

    def fill_hot(z, carry):
        ids = lax.broadcasted_iota(jnp.int32, (width, nrec), 0) + z * width
        hot[pl.ds(pl.multiple_of(z * width, width), width), :] = jnp.where(
            ids == rec_row, 1.0, 0.0).astype(jnp.bfloat16)
        return carry

    def inject_moment(k):
        col_hit = lax.broadcasted_iota(jnp.int32, (length, nrec), 0) == rec_col
        amount = res[0, k:k + 1, :]
        parts = []
        for _ in range(3):
            part = amount.astype(jnp.bfloat16).astype(jnp.float32)
            parts.append(jnp.where(col_hit, part, 0.0).astype(jnp.bfloat16))
            amount = amount - part

        def fill(z, carry):
            here = hot[pl.ds(pl.multiple_of(z * width, width), width), :]
            total = None
            for part in parts:
                product = lax.dot_general(
                    here, part, (((1,), (1,)), ((), ())),
                    preferred_element_type=jnp.float32)
                total = product if total is None else total + product
            inj[k, z] = total
            return carry

        lax.fori_loop(0, depth, fill, 0)

    lax.fori_loop(0, depth, fill_hot, 0)
    inject_moment(STEPS - 1)
    for d in range(1, zs):
        from_z_side(0, d)
    for d in range(zs):
        from_x_side(0, d)
    for copy in loads:
        copy.wait()
    finish_gather(0)

    lane = lax.broadcasted_iota(jnp.int32, (chunk, LANES), 1)

    def lateral(field, z, r0):
        def at(t, offset):
            return field[z, t, pl.ds(r0 + (PAD + offset), chunk), :]

        centre = [at(t, 0) for t in range(tiles)]

        def shifted(amount):
            turned = [pltpu.roll(t, amount % LANES, 1) for t in centre]
            result = []
            for i in range(tiles):
                if amount > 0:
                    fill = turned[i - 1] if i > 0 else 0.0
                    result.append(jnp.where(lane >= amount, turned[i], fill))
                else:
                    fill = turned[i + 1] if i + 1 < tiles else 0.0
                    result.append(jnp.where(lane < LANES + amount, turned[i], fill))
            return result

        up1, down1, up2, down2 = shifted(1), shifted(-1), shifted(2), shifted(-2)
        result = []
        for t in range(tiles):
            close = (up1[t] + down1[t]) + (at(t, 1) + at(t, -1))
            remote = (up2[t] + down2[t]) + (at(t, 2) + at(t, -2))
            result.append(C1 * close - C2 * remote - 5.0 * centre[t])
        return jnp.concatenate(centre, axis=1), jnp.concatenate(result, axis=1)

    def get_tiles(field, z, r0):
        return jnp.concatenate(
            [field[z, t, pl.ds(r0 + PAD, chunk), :] for t in range(tiles)], axis=1)

    def put_tiles(field, z, r0, value):
        for t in range(tiles):
            field[z, t, pl.ds(r0 + PAD, chunk), :] = value[:, t * LANES:(t + 1) * LANES]

    def vertical(field, z, r0):
        def at(offset):
            return field[z + (2 + offset), pl.ds(r0, chunk), :]

        centre = at(0)
        return centre, C1 * (at(1) + at(-1)) - C2 * (at(2) + at(-2)) - 2.5 * centre

    source_row = src[0] // length - first_row
    source_col = lax.rem(src[0], length)
    row_ids = lax.broadcasted_iota(jnp.int32, (chunk, length), 0)
    col_hit = lax.broadcasted_iota(jnp.int32, (1, length), 1) == source_col
    P_, Q_ = (p0, p1), (q0, q1)
    W_, S_ = (w0, w1), (s0, s1)

    def forward(k, z, r0, place=None, sub=None):
        now, old = (k + 1) % 2, k % 2
        here = (z, pl.ds(r0, chunk), slice(None))
        p_now, flat = lateral(P_[now], z, r0)
        q_now, dep = vertical(Q_[now], z, r0)
        if k + 1 < STEPS:
            st, sr = stiff[here], stretch[here]
            pulse = jnp.where(
                row_ids == source_row - (z * width + r0),
                jnp.where(col_hit, wav[0, k], 0.0), 0.0)
            layer = (z + 2, pl.ds(r0, chunk), slice(None))
            p_old, q_old = get_tiles(P_[old], z, r0), Q_[old][layer]
            p_new = 2.0 * p_now - p_old + st * (sr * flat + dep) + pulse
            q_new = 2.0 * q_now - q_old + st * (flat + dep) + pulse
            put_tiles(P_[old], z, r0, p_new)
            Q_[old][layer] = q_new
        if k == 0:
            flat0[here], dep0[here] = flat, dep
        elif k == 1:
            flat1[here], dep1[here] = flat, dep
        elif k == 2:
            a, b = a1[here], b1[here]
            img1[here] = a * flat
            img2[here] = a * dep + b * (flat + dep)
        else:
            a, b = a0[here], b0[here]
            img1[here] = img1[here] + a * flat
            img2[here] = img2[here] + (a * dep + b * (flat + dep))

    def weigh(slot, z, r0, a, b):
        here = (z, pl.ds(r0, chunk), slice(None))
        st, sr = stiff[here], stretch[here]
        put_tiles(W_[slot], z, r0, st * (sr * a + b))
        S_[slot][z + 2, pl.ds(r0, chunk), :] = st * (a + b)

    def start_adjoint(z, r0, place=None, sub=None):
        here = (z, pl.ds(r0, chunk), slice(None))
        weigh(0, z, r0, a1[here], b1[here])

    def adjoint(k, z, r0, place=None, sub=None):
        turn = STEPS - 1 - k
        old_a, now_a, new_a = ((a0, a1, a0), (a1, a0, a1), (a0, a1, a2), (a1, a2, None))[turn]
        old_b, now_b, new_b = ((b0, b1, b0), (b1, b0, b1), (b0, b1, b2), (b1, b2, None))[turn]
        here = (z, pl.ds(r0, chunk), slice(None))
        a = 2.0 * now_a[here] - old_a[here] + lateral(W_[turn % 2], z, r0)[1] + inj[(k,) + here]
        b = 2.0 * now_b[here] - old_b[here] + vertical(S_[turn % 2], z, r0)[1]
        if new_a is not None:
            new_a[here], new_b[here] = a, b
            weigh((turn + 1) % 2, z, r0, a, b)
        if k == 1:
            flat, dep = flat1[here], dep1[here]
            img1[here] = img1[here] + a * flat
            img2[here] = img2[here] + (a * dep + b * (flat + dep))
        elif k == 0:
            flat, dep = flat0[here], dep0[here]
            one = img1[here] + a * flat
            two = img2[here] + (a * dep + b * (flat + dep))
            st, sr = stiff[here], stretch[here]
            for i in range(chunk // rows):
                part = slice(i * rows, (i + 1) * rows)
                d = r0 // rows + i
                speed = gath[d, place, 0, sub]
                term[d, place, 0, sub] = 2.0 * speed * (sr[part] * one[part] + two[part])
                term[d, place, 1, sub] = 2.0 * st[part] * one[part]

    def sweep(body, g):
        low, high = groups[g]

        def turn(i, carry):
            j = i // n_chunks
            place, sub = low + j // 2, lax.rem(j, 2)
            r0 = pl.multiple_of(lax.rem(i, n_chunks) * chunk, chunk)
            body(first_layer_of(place) + sub, r0, place, sub)
            return carry

        lax.fori_loop(0, (high - low) * 2 * n_chunks, turn, 0)

    def near_sweep(body, waits=None, sends=None):
        def stripe(c, carry):
            r0 = pl.multiple_of(c * chunk, chunk)
            if waits is not None:
                wait_halo(*waits, c)

            def layer(i, inner_carry):
                body(first_layer_of(i // 2) + lax.rem(i, 2), r0)
                return inner_carry

            lax.fori_loop(0, near * 2, layer, 0)
            if sends is not None:
                send_halo(*sends, c)
            return carry

        lax.fori_loop(0, n_chunks, stripe, 0)

    near_sweep(start_adjoint, None, (s0, 4))
    if zs > 1:
        from_z_side(1, 1)
    near_sweep(functools.partial(forward, 0), (q1, 0), (q0, 1))
    for d in range(2, zs):
        from_z_side(1, d)
    inject_moment(2)
    inject_moment(1)
    for d in range(zs):
        from_x_side(1, d)
    inject_moment(0)
    finish_gather(1)
    sweep(start_adjoint, 1)
    sweep(functools.partial(forward, 0), 1)
    for turn in range(STEPS - 1):
        k = STEPS - 1 - turn
        near_sweep(functools.partial(adjoint, k), (S_[turn % 2], 4 + turn),
                   (S_[(turn + 1) % 2], 5 + turn))
        sweep(functools.partial(adjoint, k), 1)
        f = turn + 1
        if f + 1 < STEPS:
            near_sweep(functools.partial(forward, f), (Q_[(f + 1) % 2], f), (Q_[f % 2], f + 1))
            sweep(functools.partial(forward, f), 1)

    def sum_copy(g, owner, target, index, landing, send_sem, recv_sem):
        low, high = groups[g]
        places = pl.ds(low, high - low)
        return pltpu.make_async_remote_copy(
            src_ref=term.at[owner, places], dst_ref=landing.at[index, places],
            send_sem=send_sem.at[g, index], recv_sem=recv_sem.at[g, index],
            device_id={"shot": target}, device_id_type=MESH)

    def core_sum(g, j):
        return sum_copy(
            g, 2 * j + (1 - core), shot_at(zi, xi, 1 - core), j, from_core, rc_send, rc_recv)

    def x_sum(g, z):
        return sum_copy(
            g, shot_at(z, 1 - xi, core), shot_at(zi, 1 - xi, core), z, from_x,
            rx_send, rx_recv)

    def z_sum(g, d):
        owner = shot_at(lax.rem(zi + d, zs), xi, core)
        return sum_copy(g, owner, owner, d, from_z, rz_send, rz_recv)

    pairs = chunk // rows // 2

    def last(g):
        low, high = groups[g]

        def stripe(c, carry):
            r0 = pl.multiple_of(c * chunk, chunk)
            if g == 0:
                wait_halo(S_[(STEPS - 1) % 2], 3 + STEPS, c)

            def layer(i, inner_carry):
                place, sub = low + i // 2, lax.rem(i, 2)
                adjoint(0, first_layer_of(place) + sub, r0, place, sub)
                return inner_carry

            lax.fori_loop(0, (high - low) * 2, layer, 0)
            for i in range(pairs):
                core_sum(g, c * pairs + i).start()
            return carry

        lax.fori_loop(0, n_chunks, stripe, 0)

    def add(g, owner, landing, index):
        low, high = groups[g]
        places = pl.ds(low, high - low)
        term[owner, places] = term[owner, places] + landing[index, places]

    order = list(range(1, zs)) + [0]

    def sum_cores(g):
        for x, side in ((1 - xi, True), (xi, False)):
            for d in order:
                z = lax.rem(zi + d, zs)
                j = z * 2 + x
                core_sum(g, j).wait_recv()
                add(g, 2 * j + core, from_core, j)
                if side:
                    x_sum(g, z).start()

    def sum_x(g):
        for d in order:
            z = lax.rem(zi + d, zs)
            x_sum(g, z).wait_recv()
            add(g, shot_at(z, xi, core), from_x, z)
            if d > 0:
                z_sum(g, d).start()

    def sum_z(g):
        low, high = groups[g]
        for d in range(1, zs):
            z_sum(g, d).wait_recv()
        for place in range(low, high):
            total = term[me, place]
            for d in range(1, zs):
                total = total + from_z[d, place]
            pair = pl.ds(first_layer_of(place), 2)
            out[0, pair] = total[0]
            out[1, pair] = total[1]

    sweep(functools.partial(forward, STEPS - 1), 1)
    last(1)
    sum_cores(1)
    near_sweep(functools.partial(forward, STEPS - 1), (Q_[STEPS % 2], STEPS - 1))
    last(0)
    sum_x(1)
    sum_cores(0)
    sum_x(0)
    sum_z(1)
    sum_z(0)
    for g in range(2):
        for j in range(2 * zs):
            core_sum(g, j).wait_send()
        for z in range(zs):
            x_sum(g, z).wait_send()
        for d in range(1, zs):
            z_sum(g, d).wait_send()


def on_device(velocity, epsilon, forward_state, adjoint_state, source_cell, wavelet,
              receiver_cells, residuals, shots, doms):
    depth, width, length = forward_state.shape[2:]
    rows = velocity.shape[1]
    nrec = receiver_cells.shape[1]
    chunk = 64
    zs = shots // 4
    f32 = jnp.float32
    slab = pltpu.VMEM((depth, width, length), f32)
    wide = pltpu.VMEM((depth, length // LANES, width + 2 * PAD, LANES), f32)
    tall = pltpu.VMEM((depth + 4, width, length), f32)
    block = (depth // 2, 2, 2, rows, length)
    dma = pltpu.SemaphoreType.DMA
    scratch = (
        [wide] * 2 + [tall] * 2 + [wide] * 2 + [tall] * 2 + [slab] * 6
        + [slab] * 4 + [slab] * 2 + [slab] * 2
        + [pltpu.VMEM((STEPS, depth, width, length), f32),
           pltpu.VMEM((depth * width, nrec), jnp.bfloat16)]
        + [pltpu.VMEM((shots,) + block, f32), pltpu.VMEM((shots,) + block, f32),
           pltpu.VMEM((2 * zs,) + block, f32), pltpu.VMEM((zs,) + block, f32),
           pltpu.VMEM((zs,) + block, f32)]
        + [dma((6 + 2 * (length // LANES),)), dma((depth // 2, 2)),
           dma((2, zs)), dma((2, zs)), dma((2, 2 * zs)), dma((2, shots)),
           dma((2 * STEPS, 2, width // chunk)), dma((2 * STEPS, 2, width // chunk)),
           dma((2, 2 * zs)), dma((2, 2 * zs)), dma((2, zs)), dma((2, zs)),
           dma((2, zs)), dma((2, zs))]
    )
    vmem = pl.BlockSpec(memory_space=pltpu.VMEM)
    smem = pl.BlockSpec(memory_space=pltpu.SMEM)
    hbm = pl.BlockSpec(memory_space=pl.ANY)
    grads = pl.pallas_call(
        functools.partial(kernel, shots, doms, chunk),
        out_shape=jax.ShapeDtypeStruct((2, depth, rows, length), f32),
        in_specs=[hbm, hbm, hbm, hbm, smem, smem, vmem, vmem],
        out_specs=vmem,
        scratch_shapes=scratch,
        compiler_params=pltpu.CompilerParams(
            collective_id=0, has_side_effects=True, vmem_limit_bytes=56 * 2**20),
        name="vti_window",
    )(velocity, epsilon, forward_state, adjoint_state, source_cell, wavelet,
      receiver_cells, residuals)
    return (grads[0], grads[1])


def solution(mesh):
    placed = (
        P("dom", "shot", None),
        P("dom", "shot", None),
        P("shot", None, "dom", None, None),
        P("shot", None, "dom", None, None),
        P("shot"),
        P("shot", None),
        P("shot", None),
        P("shot", None, None),
    )
    return jax.shard_map(
        functools.partial(on_device, shots=mesh.shape["shot"], doms=mesh.shape["dom"]),
        mesh=mesh,
        in_specs=placed,
        out_specs=(P("dom", "shot", None), P("dom", "shot", None)),
        check_vma=False,
    )
```

```python
import functools

import jax
import jax.numpy as jnp
from jax import lax
from jax.experimental import pallas as pl
from jax.experimental.pallas import tpu as pltpu
from jax.sharding import PartitionSpec as P

STEPS = 4
PAD = 8
LANES = 128
C1, C2 = 4.0 / 3.0, 1.0 / 12.0
MESH = pl.DeviceIdType.MESH


def kernel(
    shots, doms, chunk, block,
    vel, eps, fwd, adj, src, wav, rec, res, out,
    p0, p1, q0, q1, w0, w1, s0, s1, a0, a1, a2, b0, b1, b2,
    flat0, flat1, dep0, dep1, img1, img2, stiff, stretch, inj, hot,
    gath, term, from_core, from_x, from_z,
    load_sem, own_sem, z_send, x_send, c_send, g_recv,
    halo_send, halo_recv, rc_send, rc_recv, rx_send, rx_recv, rz_send, rz_recv,
):
    depth, width, length = stiff.shape
    rows = vel.shape[1]
    nrec = rec.shape[1]
    zs = shots // 4
    me = lax.axis_index("shot")
    dom = lax.axis_index("dom")
    core = lax.rem(me, 2)
    xi = lax.rem(me // 2, 2)
    zi = me // 4
    n_chunks = width // chunk
    n_pairs = depth // 2
    near = 1 if doms == 2 else 2
    groups = ((0, near), (near, n_pairs))

    def shot_at(z, x, c):
        return (z * 2 + x) * 2 + c

    has_low = dom > 0
    has_high = dom < doms - 1

    def first_layer_of(place):
        if doms == 2:
            return 2 * jnp.where(has_low, place, n_pairs - 1 - place)
        end = jnp.where(place == 1, n_pairs - 1, place - 1)
        return 2 * jnp.where(place == 0, 0, end)

    loads = []

    def load(source, target):
        copy = pltpu.make_async_copy(source, target, load_sem.at[len(loads)])
        copy.start()
        loads.append(copy)

    own = []
    for place in range(n_pairs):
        pair = pl.ds(first_layer_of(place), 2)
        for i, model in enumerate((vel, eps)):
            copy = pltpu.make_async_copy(
                model.at[pair], gath.at[me, place, i], own_sem.at[place, i])
            copy.start()
            own.append(copy)
    inner = pl.ds(PAD, width)
    cells = pl.ds(2, depth)
    load(adj.at[0, 1], a1)
    load(adj.at[0, 3], b1)
    tiles = length // LANES
    for t in range(tiles):
        load(fwd.at[0, 1, :, :, pl.ds(t * LANES, LANES)], p1.at[:, t, inner, :])
    load(fwd.at[0, 3], q1.at[cells])
    for t in range(tiles):
        load(fwd.at[0, 0, :, :, pl.ds(t * LANES, LANES)], p0.at[:, t, inner, :])
    load(fwd.at[0, 2], q0.at[cells])
    load(adj.at[0, 0], a0)
    load(adj.at[0, 2], b0)

    barrier = pltpu.get_barrier_semaphore()
    for d in range(1, zs):
        pl.semaphore_signal(
            barrier, inc=1, device_id={"shot": shot_at(lax.rem(zi + d, zs), xi, core)},
            device_id_type=MESH)
    pl.semaphore_signal(
        barrier, inc=1, device_id={"shot": shot_at(zi, 1 - xi, core)}, device_id_type=MESH)
    pl.semaphore_signal(
        barrier, inc=1, device_id={"shot": shot_at(zi, xi, 1 - core)}, device_id_type=MESH)

    @pl.when(has_low)
    def _():
        pl.semaphore_signal(barrier, inc=1, device_id={"dom": dom - 1}, device_id_type=MESH)

    @pl.when(has_high)
    def _():
        pl.semaphore_signal(barrier, inc=1, device_id={"dom": dom + 1}, device_id_type=MESH)

    beside = jnp.where(has_low, 1, 0) + jnp.where(has_high, 1, 0)
    pl.semaphore_wait(barrier, zs + 1 + beside)

    def low_copy(source, field, slot, c):
        stripe = pl.ds(pl.multiple_of(c * chunk, chunk), chunk)
        return pltpu.make_async_remote_copy(
            src_ref=source.at[:, stripe, :], dst_ref=field.at[pl.ds(depth + 2, 2), stripe, :],
            send_sem=halo_send.at[slot, 0, c], recv_sem=halo_recv.at[slot, 1, c],
            device_id={"dom": dom - 1}, device_id_type=MESH)

    def high_copy(source, field, slot, c):
        stripe = pl.ds(pl.multiple_of(c * chunk, chunk), chunk)
        return pltpu.make_async_remote_copy(
            src_ref=source.at[:, stripe, :], dst_ref=field.at[pl.ds(0, 2), stripe, :],
            send_sem=halo_send.at[slot, 1, c], recv_sem=halo_recv.at[slot, 0, c],
            device_id={"dom": dom + 1}, device_id_type=MESH)

    def send_halo(field, slot, c, low=None, high=None):
        low = field.at[pl.ds(2, 2)] if low is None else low
        high = field.at[pl.ds(depth, 2)] if high is None else high

        @pl.when(has_low)
        def _():
            low_copy(low, field, slot, c).start()

        @pl.when(has_high)
        def _():
            high_copy(high, field, slot, c).start()

    def wait_halo(field, slot, c):
        low, high = field.at[pl.ds(2, 2)], field.at[pl.ds(depth, 2)]

        @pl.when(has_low)
        def _():
            low_copy(low, field, slot, c).wait_send()
            high_copy(high, field, slot, c).wait_recv()

        @pl.when(has_high)
        def _():
            high_copy(high, field, slot, c).wait_send()
            low_copy(low, field, slot, c).wait_recv()

    for c in range(n_chunks):
        send_halo(
            q1, 0, c, fwd.at[0, 3, pl.ds(0, 2)], fwd.at[0, 3, pl.ds(depth - 2, 2)])

    def block_copy(g, owner, target, send_sem):
        low, high = groups[g]
        part = gath.at[owner, pl.ds(low, high - low)]
        return pltpu.make_async_remote_copy(
            src_ref=part, dst_ref=part, send_sem=send_sem, recv_sem=g_recv.at[g, owner],
            device_id={"shot": target}, device_id_type=MESH)

    def to_x(g, z):
        return block_copy(
            g, shot_at(z, xi, core), shot_at(zi, 1 - xi, core), x_send.at[g, z])

    def to_core(g, z, x):
        return block_copy(
            g, shot_at(z, x, core), shot_at(zi, xi, 1 - core), c_send.at[g, z * 2 + x])

    def to_z(g, d):
        return block_copy(
            g, me, shot_at(lax.rem(zi + d, zs), xi, core), z_send.at[g, d])

    def arrived(g, owner):
        block_copy(g, owner, me, x_send.at[g, 0]).wait_recv()

    def from_z_side(g, d):
        other = lax.rem(zi + (zs - d), zs)
        arrived(g, shot_at(other, xi, core))
        to_x(g, other).start()
        to_core(g, other, xi).start()

    def from_x_side(g, d):
        other = lax.rem(zi + (zs - d), zs)
        arrived(g, shot_at(other, 1 - xi, core))
        to_core(g, other, 1 - xi).start()

    def finish_gather(g):
        for z in range(zs):
            for x in range(2):
                arrived(g, shot_at(z, x, 1 - core))
        for d in range(1, zs):
            to_z(g, d).wait_send()
        for z in range(zs):
            to_x(g, z).wait_send()
            for x in range(2):
                to_core(g, z, x).wait_send()

        def spread(place, carry):
            pair = pl.ds(first_layer_of(place), 2)
            for s in range(shots):
                part = slice(s * rows, (s + 1) * rows)
                speed = gath[s, place, 0]
                stiff[pair, part, :] = speed * speed
                stretch[pair, part, :] = 1.0 + 2.0 * gath[s, place, 1]
            return carry

        lax.fori_loop(*groups[g], spread, 0)

    for copy in own:
        copy.wait()
    for g in range(2):
        to_x(g, zi).start()
        for d in range(1, zs):
            to_z(g, d).start()
        to_core(g, zi, xi).start()

    edge = jnp.zeros((depth, tiles, PAD, LANES), jnp.float32)
    for field in (p0, p1, w0, w1):
        field[:, :, 0:PAD, :] = edge
        field[:, :, PAD + width:PAD + width + PAD, :] = edge
    halo = jnp.zeros((2, width, length), jnp.float32)

    @pl.when(dom == 0)
    def _():
        for field in (q0, q1, s0, s1):
            field[0:2] = halo

    @pl.when(dom == doms - 1)
    def _():
        for field in (q0, q1, s0, s1):
            field[depth + 2:depth + 4] = halo

    first_row = dom * (depth * width)
    rec_row = rec[...] // length - first_row
    rec_col = lax.rem(rec[...], length)
    all_rows = depth * width

    def fill_hot(z, carry):
        ids = lax.broadcasted_iota(jnp.int32, (width, nrec), 0) + z * width
        hot[pl.ds(pl.multiple_of(z * width, width), width), :] = jnp.where(
            ids == rec_row, 1.0, 0.0).astype(jnp.bfloat16)
        return carry

    span = depth // 2

    def inject_moment(k):
        col_hit = lax.broadcasted_iota(jnp.int32, (length, nrec), 0) == rec_col
        amount = res[0, k:k + 1, :]
        parts = []
        for _ in range(3):
            part = amount.astype(jnp.bfloat16).astype(jnp.float32)
            parts.append(jnp.where(col_hit, part, 0.0).astype(jnp.bfloat16))
            amount = amount - part

        def fill(i, carry):
            here = hot[pl.ds(pl.multiple_of(i * span * width, width), span * width), :]
            total = None
            for part in parts:
                product = lax.dot_general(
                    here, part, (((1,), (1,)), ((), ())),
                    preferred_element_type=jnp.float32)
                total = product if total is None else total + product
            inj[k, pl.ds(i * span, span)] = total.reshape(span, width, length)
            return carry

        lax.fori_loop(0, depth // span, fill, 0)

    lax.fori_loop(0, depth, fill_hot, 0)
    inject_moment(STEPS - 1)
    for d in range(1, zs):
        from_z_side(0, d)
    for d in range(zs):
        from_x_side(0, d)
    for copy in loads:
        copy.wait()
    finish_gather(0)

    lane = lax.broadcasted_iota(jnp.int32, (block, LANES), 1)

    def lateral(field, z, r0):
        def at(t, offset):
            return field[z, t, pl.ds(r0 + (PAD + offset), block), :]

        centre = [at(t, 0) for t in range(tiles)]

        def shifted(amount):
            turned = [pltpu.roll(t, amount % LANES, 1) for t in centre]
            result = []
            for i in range(tiles):
                if amount > 0:
                    fill = turned[i - 1] if i > 0 else 0.0
                    result.append(jnp.where(lane >= amount, turned[i], fill))
                else:
                    fill = turned[i + 1] if i + 1 < tiles else 0.0
                    result.append(jnp.where(lane < LANES + amount, turned[i], fill))
            return result

        up1, down1, up2, down2 = shifted(1), shifted(-1), shifted(2), shifted(-2)
        result = []
        for t in range(tiles):
            close = (up1[t] + down1[t]) + (at(t, 1) + at(t, -1))
            remote = (up2[t] + down2[t]) + (at(t, 2) + at(t, -2))
            result.append(C1 * close - C2 * remote - 5.0 * centre[t])
        return jnp.concatenate(centre, axis=1), jnp.concatenate(result, axis=1)

    def get_tiles(field, z, r0):
        return jnp.concatenate(
            [field[z, t, pl.ds(r0 + PAD, block), :] for t in range(tiles)], axis=1)

    def put_tiles(field, z, r0, value):
        for t in range(tiles):
            field[z, t, pl.ds(r0 + PAD, block), :] = value[:, t * LANES:(t + 1) * LANES]

    def vertical(field, z, r0):
        def at(offset):
            return field[z + (2 + offset), pl.ds(r0, block), :]

        centre = at(0)
        return centre, C1 * (at(1) + at(-1)) - C2 * (at(2) + at(-2)) - 2.5 * centre

    source_row = src[0] // length - first_row
    source_col = lax.rem(src[0], length)
    row_ids = lax.broadcasted_iota(jnp.int32, (block, length), 0)
    col_hit = lax.broadcasted_iota(jnp.int32, (1, length), 1) == source_col
    P_, Q_ = (p0, p1), (q0, q1)
    W_, S_ = (w0, w1), (s0, s1)

    def forward(k, z, r0, place=None, sub=None):
        now, old = (k + 1) % 2, k % 2
        here = (z, pl.ds(r0, block), slice(None))
        p_now, flat = lateral(P_[now], z, r0)
        q_now, dep = vertical(Q_[now], z, r0)
        if k + 1 < STEPS:
            st, sr = stiff[here], stretch[here]
            pulse = jnp.where(
                row_ids == source_row - (z * width + r0),
                jnp.where(col_hit, wav[0, k], 0.0), 0.0)
            layer = (z + 2, pl.ds(r0, block), slice(None))
            p_old, q_old = get_tiles(P_[old], z, r0), Q_[old][layer]
            p_new = 2.0 * p_now - p_old + st * (sr * flat + dep) + pulse
            q_new = 2.0 * q_now - q_old + st * (flat + dep) + pulse
        if k >= 2:
            a, b = (a1[here], b1[here]) if k == 2 else (a0[here], b0[here])
            one, two = a * flat, a * dep + b * (flat + dep)
            if k > 2:
                one, two = img1[here] + one, img2[here] + two

        def commit():
            if k + 1 < STEPS:
                put_tiles(P_[old], z, r0, p_new)
                Q_[old][layer] = q_new
            if k == 0:
                flat0[here], dep0[here] = flat, dep
            elif k == 1:
                flat1[here], dep1[here] = flat, dep
            else:
                img1[here], img2[here] = one, two

        return commit

    def weigh(slot, z, r0, a, b):
        here = (z, pl.ds(r0, block), slice(None))
        st, sr = stiff[here], stretch[here]
        weighed, plain = st * (sr * a + b), st * (a + b)

        def commit():
            put_tiles(W_[slot], z, r0, weighed)
            S_[slot][z + 2, pl.ds(r0, block), :] = plain

        return commit

    def start_adjoint(z, r0, place=None, sub=None):
        here = (z, pl.ds(r0, block), slice(None))
        return weigh(0, z, r0, a1[here], b1[here])

    def adjoint(k, z, r0, place=None, sub=None):
        turn = STEPS - 1 - k
        old_a, now_a, new_a = ((a0, a1, a0), (a1, a0, a1), (a0, a1, a2), (a1, a2, None))[turn]
        old_b, now_b, new_b = ((b0, b1, b0), (b1, b0, b1), (b0, b1, b2), (b1, b2, None))[turn]
        here = (z, pl.ds(r0, block), slice(None))
        a = 2.0 * now_a[here] - old_a[here] + lateral(W_[turn % 2], z, r0)[1] + inj[(k,) + here]
        b = 2.0 * now_b[here] - old_b[here] + vertical(S_[turn % 2], z, r0)[1]
        commit_weighed = None
        if new_a is not None:
            commit_weighed = weigh((turn + 1) % 2, z, r0, a, b)
        if k == 1:
            flat, dep = flat1[here], dep1[here]
            one = img1[here] + a * flat
            two = img2[here] + (a * dep + b * (flat + dep))
        elif k == 0:
            flat, dep = flat0[here], dep0[here]
            one = img1[here] + a * flat
            two = img2[here] + (a * dep + b * (flat + dep))
            st, sr = stiff[here], stretch[here]
            first = 2.0 * (sr * one + two)
            second = 2.0 * st * one
            speeds = [gath[r0 // rows + i, place, 0, sub] for i in range(block // rows)]

        def commit():
            if new_a is not None:
                new_a[here], new_b[here] = a, b
                commit_weighed()
            if k == 1:
                img1[here], img2[here] = one, two
            elif k == 0:
                for i, speed in enumerate(speeds):
                    part = slice(i * rows, (i + 1) * rows)
                    term[r0 // rows + i, place, 0, sub] = speed * first[part]
                    term[r0 // rows + i, place, 1, sub] = second[part]

        return commit

    def run(body, z, r0, place=None, sub=None):
        pending = None
        for i in range(chunk // block):
            commit = body(z, pl.multiple_of(r0 + i * block, block), place, sub)
            if pending is not None:
                pending()
            pending = commit
        pending()

    def sweep(body, g):
        low, high = groups[g]

        def turn(i, carry):
            j = i // n_chunks
            place, sub = low + j // 2, lax.rem(j, 2)
            r0 = pl.multiple_of(lax.rem(i, n_chunks) * chunk, chunk)
            run(body, first_layer_of(place) + sub, r0, place, sub)
            return carry

        lax.fori_loop(0, (high - low) * 2 * n_chunks, turn, 0)

    def near_sweep(body, waits=None, sends=None):
        def stripe(c, carry):
            r0 = pl.multiple_of(c * chunk, chunk)
            if waits is not None:
                wait_halo(*waits, c)

            def layer(i, inner_carry):
                run(body, first_layer_of(i // 2) + lax.rem(i, 2), r0)
                return inner_carry

            lax.fori_loop(0, near * 2, layer, 0)
            if sends is not None:
                send_halo(*sends, c)
            return carry

        lax.fori_loop(0, n_chunks, stripe, 0)

    near_sweep(start_adjoint, None, (s0, 4))
    if zs > 1:
        from_z_side(1, 1)
    near_sweep(functools.partial(forward, 0), (q1, 0), (q0, 1))
    for d in range(2, zs):
        from_z_side(1, d)
    inject_moment(2)
    inject_moment(1)
    for d in range(zs):
        from_x_side(1, d)
    inject_moment(0)
    finish_gather(1)
    sweep(start_adjoint, 1)
    sweep(functools.partial(forward, 0), 1)
    for turn in range(STEPS - 1):
        k = STEPS - 1 - turn
        near_sweep(functools.partial(adjoint, k), (S_[turn % 2], 4 + turn),
                   (S_[(turn + 1) % 2], 5 + turn))
        sweep(functools.partial(adjoint, k), 1)
        f = turn + 1
        if f + 1 < STEPS:
            near_sweep(functools.partial(forward, f), (Q_[(f + 1) % 2], f), (Q_[f % 2], f + 1))
            sweep(functools.partial(forward, f), 1)

    def sum_copy(g, owner, target, index, landing, send_sem, recv_sem):
        low, high = groups[g]
        places = pl.ds(low, high - low)
        return pltpu.make_async_remote_copy(
            src_ref=term.at[owner, places], dst_ref=landing.at[index, places],
            send_sem=send_sem.at[g, index], recv_sem=recv_sem.at[g, index],
            device_id={"shot": target}, device_id_type=MESH)

    def core_sum(g, j):
        return sum_copy(
            g, 2 * j + (1 - core), shot_at(zi, xi, 1 - core), j, from_core, rc_send, rc_recv)

    def x_sum(g, z):
        return sum_copy(
            g, shot_at(z, 1 - xi, core), shot_at(zi, 1 - xi, core), z, from_x,
            rx_send, rx_recv)

    def z_sum(g, d):
        owner = shot_at(lax.rem(zi + d, zs), xi, core)
        return sum_copy(g, owner, owner, d, from_z, rz_send, rz_recv)

    pairs = chunk // rows // 2

    def last(g):
        low, high = groups[g]

        def stripe(c, carry):
            r0 = pl.multiple_of(c * chunk, chunk)
            if g == 0:
                wait_halo(S_[(STEPS - 1) % 2], 3 + STEPS, c)

            def layer(i, inner_carry):
                place, sub = low + i // 2, lax.rem(i, 2)
                run(functools.partial(adjoint, 0), first_layer_of(place) + sub, r0, place, sub)
                return inner_carry

            lax.fori_loop(0, (high - low) * 2, layer, 0)
            for i in range(pairs):
                core_sum(g, c * pairs + i).start()
            return carry

        lax.fori_loop(0, n_chunks, stripe, 0)

    def add(g, owner, landing, index):
        low, high = groups[g]
        places = pl.ds(low, high - low)
        term[owner, places] = term[owner, places] + landing[index, places]

    order = list(range(1, zs)) + [0]

    def sum_cores(g):
        for x, side in ((1 - xi, True), (xi, False)):
            for d in order:
                z = lax.rem(zi + d, zs)
                j = z * 2 + x
                core_sum(g, j).wait_recv()
                add(g, 2 * j + core, from_core, j)
                if side:
                    x_sum(g, z).start()

    def sum_x(g):
        for d in order:
            z = lax.rem(zi + d, zs)
            x_sum(g, z).wait_recv()
            add(g, shot_at(z, xi, core), from_x, z)
            if d > 0:
                z_sum(g, d).start()

    def sum_z(g):
        low, high = groups[g]
        for d in range(1, zs):
            z_sum(g, d).wait_recv()
        for place in range(low, high):
            total = term[me, place]
            for d in range(1, zs):
                total = total + from_z[d, place]
            pair = pl.ds(first_layer_of(place), 2)
            out[0, pair] = total[0]
            out[1, pair] = total[1]

    sweep(functools.partial(forward, STEPS - 1), 1)
    last(1)
    sum_cores(1)
    near_sweep(functools.partial(forward, STEPS - 1), (Q_[STEPS % 2], STEPS - 1))
    last(0)
    sum_x(1)
    sum_cores(0)
    sum_x(0)
    sum_z(1)
    sum_z(0)
    for g in range(2):
        for j in range(2 * zs):
            core_sum(g, j).wait_send()
        for z in range(zs):
            x_sum(g, z).wait_send()
        for d in range(1, zs):
            z_sum(g, d).wait_send()


def on_device(velocity, epsilon, forward_state, adjoint_state, source_cell, wavelet,
              receiver_cells, residuals, shots, doms):
    depth, width, length = forward_state.shape[2:]
    rows = velocity.shape[1]
    nrec = receiver_cells.shape[1]
    chunk = 64
    zs = shots // 4
    f32 = jnp.float32
    slab = pltpu.VMEM((depth, width, length), f32)
    wide = pltpu.VMEM((depth, length // LANES, width + 2 * PAD, LANES), f32)
    tall = pltpu.VMEM((depth + 4, width, length), f32)
    block = (depth // 2, 2, 2, rows, length)
    dma = pltpu.SemaphoreType.DMA
    scratch = (
        [wide] * 2 + [tall] * 2 + [wide] * 2 + [tall] * 2 + [slab] * 6
        + [slab] * 4 + [slab] * 2 + [slab] * 2
        + [pltpu.VMEM((STEPS, depth, width, length), f32),
           pltpu.VMEM((depth * width, nrec), jnp.bfloat16)]
        + [pltpu.VMEM((shots,) + block, f32), pltpu.VMEM((shots,) + block, f32),
           pltpu.VMEM((2 * zs,) + block, f32), pltpu.VMEM((zs,) + block, f32),
           pltpu.VMEM((zs,) + block, f32)]
        + [dma((6 + 2 * (length // LANES),)), dma((depth // 2, 2)),
           dma((2, zs)), dma((2, zs)), dma((2, 2 * zs)), dma((2, shots)),
           dma((2 * STEPS, 2, width // chunk)), dma((2 * STEPS, 2, width // chunk)),
           dma((2, 2 * zs)), dma((2, 2 * zs)), dma((2, zs)), dma((2, zs)),
           dma((2, zs)), dma((2, zs))]
    )
    vmem = pl.BlockSpec(memory_space=pltpu.VMEM)
    smem = pl.BlockSpec(memory_space=pltpu.SMEM)
    hbm = pl.BlockSpec(memory_space=pl.ANY)
    grads = pl.pallas_call(
        functools.partial(kernel, shots, doms, chunk, 16),
        out_shape=jax.ShapeDtypeStruct((2, depth, rows, length), f32),
        in_specs=[hbm, hbm, hbm, hbm, smem, smem, vmem, vmem],
        out_specs=vmem,
        scratch_shapes=scratch,
        compiler_params=pltpu.CompilerParams(
            collective_id=0, has_side_effects=True, vmem_limit_bytes=56 * 2**20),
        name="vti_window",
    )(velocity, epsilon, forward_state, adjoint_state, source_cell, wavelet,
      receiver_cells, residuals)
    return (grads[0], grads[1])


def solution(mesh):
    placed = (
        P("dom", "shot", None),
        P("dom", "shot", None),
        P("shot", None, "dom", None, None),
        P("shot", None, "dom", None, None),
        P("shot"),
        P("shot", None),
        P("shot", None),
        P("shot", None, None),
    )
    return jax.shard_map(
        functools.partial(on_device, shots=mesh.shape["shot"], doms=mesh.shape["dom"]),
        mesh=mesh,
        in_specs=placed,
        out_specs=(P("dom", "shot", None), P("dom", "shot", None)),
        check_vma=False,
    )
```

```python
import functools

import jax
import jax.numpy as jnp
from jax import lax
from jax.experimental import pallas as pl
from jax.experimental.pallas import tpu as pltpu
from jax.sharding import PartitionSpec as P

STEPS = 4
PAD = 8
LANES = 128
C1, C2 = 4.0 / 3.0, 1.0 / 12.0
MESH = pl.DeviceIdType.MESH


def kernel(
    shots, doms, chunk, block,
    vel, eps, fwd, adj, src, wav, rec, res, out,
    p0, p1, q0, q1, w0, w1, s0, s1, a0, a1, a2, b0, b1, b2,
    flat0, flat1, dep0, dep1, img1, img2, stiff, stretch, inj, hot,
    gath, term, from_core, from_x, from_z,
    load_sem, own_sem, z_send, x_send, c_send, g_recv,
    halo_send, halo_recv, rc_send, rc_recv, rx_send, rx_recv, rz_send, rz_recv,
):
    depth, width, length = stiff.shape
    rows = vel.shape[1]
    nrec = rec.shape[1]
    zs = shots // 4
    me = lax.axis_index("shot")
    dom = lax.axis_index("dom")
    core = lax.rem(me, 2)
    xi = lax.rem(me // 2, 2)
    zi = me // 4
    n_chunks = width // chunk
    n_pairs = depth // 2
    near = 1 if doms == 2 else 2
    groups = ((0, near), (near, n_pairs))
    rounds = ((0, near + 1), (near + 1, n_pairs))

    def shot_at(z, x, c):
        return (z * 2 + x) * 2 + c

    has_low = dom > 0
    has_high = dom < doms - 1

    def first_layer_of(place):
        if doms == 2:
            return 2 * jnp.where(has_low, place, n_pairs - 1 - place)
        end = jnp.where(place == 1, n_pairs - 1, place - 1)
        return 2 * jnp.where(place == 0, 0, end)

    loads = []

    def load(source, target):
        copy = pltpu.make_async_copy(source, target, load_sem.at[len(loads)])
        copy.start()
        loads.append(copy)

    own = []
    for place in range(n_pairs):
        pair = pl.ds(first_layer_of(place), 2)
        for i, model in enumerate((vel, eps)):
            copy = pltpu.make_async_copy(
                model.at[pair], gath.at[me, place, i], own_sem.at[place, i])
            copy.start()
            own.append(copy)
    inner = pl.ds(PAD, width)
    cells = pl.ds(2, depth)
    load(adj.at[0, 1], a1)
    load(adj.at[0, 3], b1)
    tiles = length // LANES
    for t in range(tiles):
        load(fwd.at[0, 1, :, :, pl.ds(t * LANES, LANES)], p1.at[:, t, inner, :])
    load(fwd.at[0, 3], q1.at[cells])
    for t in range(tiles):
        load(fwd.at[0, 0, :, :, pl.ds(t * LANES, LANES)], p0.at[:, t, inner, :])
    load(fwd.at[0, 2], q0.at[cells])
    load(adj.at[0, 0], a0)
    load(adj.at[0, 2], b0)

    barrier = pltpu.get_barrier_semaphore()
    for d in range(1, zs):
        pl.semaphore_signal(
            barrier, inc=1, device_id={"shot": shot_at(lax.rem(zi + d, zs), xi, core)},
            device_id_type=MESH)
    pl.semaphore_signal(
        barrier, inc=1, device_id={"shot": shot_at(zi, 1 - xi, core)}, device_id_type=MESH)
    pl.semaphore_signal(
        barrier, inc=1, device_id={"shot": shot_at(zi, xi, 1 - core)}, device_id_type=MESH)

    @pl.when(has_low)
    def _():
        pl.semaphore_signal(barrier, inc=1, device_id={"dom": dom - 1}, device_id_type=MESH)

    @pl.when(has_high)
    def _():
        pl.semaphore_signal(barrier, inc=1, device_id={"dom": dom + 1}, device_id_type=MESH)

    beside = jnp.where(has_low, 1, 0) + jnp.where(has_high, 1, 0)
    pl.semaphore_wait(barrier, zs + 1 + beside)

    def low_copy(source, field, slot, c):
        stripe = pl.ds(pl.multiple_of(c * chunk, chunk), chunk)
        return pltpu.make_async_remote_copy(
            src_ref=source.at[:, stripe, :], dst_ref=field.at[pl.ds(depth + 2, 2), stripe, :],
            send_sem=halo_send.at[slot, 0, c], recv_sem=halo_recv.at[slot, 1, c],
            device_id={"dom": dom - 1}, device_id_type=MESH)

    def high_copy(source, field, slot, c):
        stripe = pl.ds(pl.multiple_of(c * chunk, chunk), chunk)
        return pltpu.make_async_remote_copy(
            src_ref=source.at[:, stripe, :], dst_ref=field.at[pl.ds(0, 2), stripe, :],
            send_sem=halo_send.at[slot, 1, c], recv_sem=halo_recv.at[slot, 0, c],
            device_id={"dom": dom + 1}, device_id_type=MESH)

    def send_halo(field, slot, c, low=None, high=None):
        low = field.at[pl.ds(2, 2)] if low is None else low
        high = field.at[pl.ds(depth, 2)] if high is None else high

        @pl.when(has_low)
        def _():
            low_copy(low, field, slot, c).start()

        @pl.when(has_high)
        def _():
            high_copy(high, field, slot, c).start()

    def wait_halo(field, slot, c):
        low, high = field.at[pl.ds(2, 2)], field.at[pl.ds(depth, 2)]

        @pl.when(has_low)
        def _():
            low_copy(low, field, slot, c).wait_send()
            high_copy(high, field, slot, c).wait_recv()

        @pl.when(has_high)
        def _():
            high_copy(high, field, slot, c).wait_send()
            low_copy(low, field, slot, c).wait_recv()

    for c in range(n_chunks):
        send_halo(
            q1, 0, c, fwd.at[0, 3, pl.ds(0, 2)], fwd.at[0, 3, pl.ds(depth - 2, 2)])

    def block_copy(g, owner, target, send_sem):
        low, high = rounds[g]
        part = gath.at[owner, pl.ds(low, high - low)]
        return pltpu.make_async_remote_copy(
            src_ref=part, dst_ref=part, send_sem=send_sem, recv_sem=g_recv.at[g, owner],
            device_id={"shot": target}, device_id_type=MESH)

    def to_x(g, z):
        return block_copy(
            g, shot_at(z, xi, core), shot_at(zi, 1 - xi, core), x_send.at[g, z])

    def to_core(g, z, x):
        return block_copy(
            g, shot_at(z, x, core), shot_at(zi, xi, 1 - core), c_send.at[g, z * 2 + x])

    def to_z(g, d):
        return block_copy(
            g, me, shot_at(lax.rem(zi + d, zs), xi, core), z_send.at[g, d])

    def arrived(g, owner):
        block_copy(g, owner, me, x_send.at[g, 0]).wait_recv()

    def from_z_side(g, d):
        other = lax.rem(zi + (zs - d), zs)
        arrived(g, shot_at(other, xi, core))
        to_x(g, other).start()
        to_core(g, other, xi).start()

    def from_x_side(g, d):
        other = lax.rem(zi + (zs - d), zs)
        arrived(g, shot_at(other, 1 - xi, core))
        to_core(g, other, 1 - xi).start()

    def finish_gather(g):
        for z in range(zs):
            for x in range(2):
                arrived(g, shot_at(z, x, 1 - core))
        for d in range(1, zs):
            to_z(g, d).wait_send()
        for z in range(zs):
            to_x(g, z).wait_send()
            for x in range(2):
                to_core(g, z, x).wait_send()

        def spread(place, carry):
            pair = pl.ds(first_layer_of(place), 2)
            for s in range(shots):
                part = slice(s * rows, (s + 1) * rows)
                speed = gath[s, place, 0]
                stiff[pair, part, :] = speed * speed
                stretch[pair, part, :] = 1.0 + 2.0 * gath[s, place, 1]
            return carry

        lax.fori_loop(*rounds[g], spread, 0)

    for copy in own:
        copy.wait()
    for g in range(2):
        to_x(g, zi).start()
        for d in range(1, zs):
            to_z(g, d).start()
        to_core(g, zi, xi).start()

    edge = jnp.zeros((depth, tiles, PAD, LANES), jnp.float32)
    for field in (p0, p1, w0, w1):
        field[:, :, 0:PAD, :] = edge
        field[:, :, PAD + width:PAD + width + PAD, :] = edge
    halo = jnp.zeros((2, width, length), jnp.float32)

    @pl.when(dom == 0)
    def _():
        for field in (q0, q1, s0, s1):
            field[0:2] = halo

    @pl.when(dom == doms - 1)
    def _():
        for field in (q0, q1, s0, s1):
            field[depth + 2:depth + 4] = halo

    first_row = dom * (depth * width)
    rec_row = rec[...] // length - first_row
    rec_col = lax.rem(rec[...], length)
    all_rows = depth * width

    def fill_hot(z, carry):
        ids = lax.broadcasted_iota(jnp.int32, (width, nrec), 0) + z * width
        hot[pl.ds(pl.multiple_of(z * width, width), width), :] = jnp.where(
            ids == rec_row, 1.0, 0.0).astype(jnp.bfloat16)
        return carry

    span = depth // 2

    def inject_moment(k):
        col_hit = lax.broadcasted_iota(jnp.int32, (length, nrec), 0) == rec_col
        amount = res[0, k:k + 1, :]
        parts = []
        for _ in range(3):
            part = amount.astype(jnp.bfloat16).astype(jnp.float32)
            parts.append(jnp.where(col_hit, part, 0.0).astype(jnp.bfloat16))
            amount = amount - part

        def fill(i, carry):
            here = hot[pl.ds(pl.multiple_of(i * span * width, width), span * width), :]
            total = None
            for part in parts:
                product = lax.dot_general(
                    here, part, (((1,), (1,)), ((), ())),
                    preferred_element_type=jnp.float32)
                total = product if total is None else total + product
            inj[k, pl.ds(i * span, span)] = total.reshape(span, width, length)
            return carry

        lax.fori_loop(0, depth // span, fill, 0)

    lax.fori_loop(0, depth, fill_hot, 0)
    inject_moment(STEPS - 1)
    for d in range(1, zs):
        from_z_side(0, d)
    for d in range(zs):
        from_x_side(0, d)
    for copy in loads:
        copy.wait()
    finish_gather(0)

    lane = lax.broadcasted_iota(jnp.int32, (block, LANES), 1)

    def lateral(field, z, r0):
        def at(t, offset):
            return field[z, t, pl.ds(r0 + (PAD + offset), block), :]

        centre = [at(t, 0) for t in range(tiles)]

        def shifted(amount):
            turned = [pltpu.roll(t, amount % LANES, 1) for t in centre]
            result = []
            for i in range(tiles):
                if amount > 0:
                    fill = turned[i - 1] if i > 0 else 0.0
                    result.append(jnp.where(lane >= amount, turned[i], fill))
                else:
                    fill = turned[i + 1] if i + 1 < tiles else 0.0
                    result.append(jnp.where(lane < LANES + amount, turned[i], fill))
            return result

        up1, down1, up2, down2 = shifted(1), shifted(-1), shifted(2), shifted(-2)
        result = []
        for t in range(tiles):
            close = (up1[t] + down1[t]) + (at(t, 1) + at(t, -1))
            remote = (up2[t] + down2[t]) + (at(t, 2) + at(t, -2))
            result.append(C1 * close - C2 * remote - 5.0 * centre[t])
        return jnp.concatenate(centre, axis=1), jnp.concatenate(result, axis=1)

    def get_tiles(field, z, r0):
        return jnp.concatenate(
            [field[z, t, pl.ds(r0 + PAD, block), :] for t in range(tiles)], axis=1)

    def put_tiles(field, z, r0, value):
        for t in range(tiles):
            field[z, t, pl.ds(r0 + PAD, block), :] = value[:, t * LANES:(t + 1) * LANES]

    def vertical(field, z, r0):
        def at(offset):
            return field[z + (2 + offset), pl.ds(r0, block), :]

        centre = at(0)
        return centre, C1 * (at(1) + at(-1)) - C2 * (at(2) + at(-2)) - 2.5 * centre

    source_row = src[0] // length - first_row
    source_col = lax.rem(src[0], length)
    row_ids = lax.broadcasted_iota(jnp.int32, (block, length), 0)
    col_hit = lax.broadcasted_iota(jnp.int32, (1, length), 1) == source_col
    P_, Q_ = (p0, p1), (q0, q1)
    W_, S_ = (w0, w1), (s0, s1)

    def forward(k, z, r0, place=None, sub=None):
        now, old = (k + 1) % 2, k % 2
        here = (z, pl.ds(r0, block), slice(None))
        p_now, flat = lateral(P_[now], z, r0)
        q_now, dep = vertical(Q_[now], z, r0)
        if k + 1 < STEPS:
            st, sr = stiff[here], stretch[here]
            pulse = jnp.where(
                row_ids == source_row - (z * width + r0),
                jnp.where(col_hit, wav[0, k], 0.0), 0.0)
            layer = (z + 2, pl.ds(r0, block), slice(None))
            p_old, q_old = get_tiles(P_[old], z, r0), Q_[old][layer]
            p_new = 2.0 * p_now - p_old + st * (sr * flat + dep) + pulse
            q_new = 2.0 * q_now - q_old + st * (flat + dep) + pulse
        if k >= 2:
            a, b = (a1[here], b1[here]) if k == 2 else (a0[here], b0[here])
            one, two = a * flat, a * dep + b * (flat + dep)
            if k > 2:
                one, two = img1[here] + one, img2[here] + two

        def commit():
            if k + 1 < STEPS:
                put_tiles(P_[old], z, r0, p_new)
                Q_[old][layer] = q_new
            if k == 0:
                flat0[here], dep0[here] = flat, dep
            elif k == 1:
                flat1[here], dep1[here] = flat, dep
            else:
                img1[here], img2[here] = one, two

        return commit

    def weigh(slot, z, r0, a, b):
        here = (z, pl.ds(r0, block), slice(None))
        st, sr = stiff[here], stretch[here]
        weighed, plain = st * (sr * a + b), st * (a + b)

        def commit():
            put_tiles(W_[slot], z, r0, weighed)
            S_[slot][z + 2, pl.ds(r0, block), :] = plain

        return commit

    def start_adjoint(z, r0, place=None, sub=None):
        here = (z, pl.ds(r0, block), slice(None))
        return weigh(0, z, r0, a1[here], b1[here])

    def adjoint(k, z, r0, place=None, sub=None):
        turn = STEPS - 1 - k
        old_a, now_a, new_a = ((a0, a1, a0), (a1, a0, a1), (a0, a1, a2), (a1, a2, None))[turn]
        old_b, now_b, new_b = ((b0, b1, b0), (b1, b0, b1), (b0, b1, b2), (b1, b2, None))[turn]
        here = (z, pl.ds(r0, block), slice(None))
        a = 2.0 * now_a[here] - old_a[here] + lateral(W_[turn % 2], z, r0)[1] + inj[(k,) + here]
        b = 2.0 * now_b[here] - old_b[here] + vertical(S_[turn % 2], z, r0)[1]
        commit_weighed = None
        if new_a is not None:
            commit_weighed = weigh((turn + 1) % 2, z, r0, a, b)
        if k == 1:
            flat, dep = flat1[here], dep1[here]
            one = img1[here] + a * flat
            two = img2[here] + (a * dep + b * (flat + dep))
        elif k == 0:
            flat, dep = flat0[here], dep0[here]
            one = img1[here] + a * flat
            two = img2[here] + (a * dep + b * (flat + dep))
            st, sr = stiff[here], stretch[here]
            first = 2.0 * (sr * one + two)
            second = 2.0 * st * one
            speeds = [gath[r0 // rows + i, place, 0, sub] for i in range(block // rows)]

        def commit():
            if new_a is not None:
                new_a[here], new_b[here] = a, b
                commit_weighed()
            if k == 1:
                img1[here], img2[here] = one, two
            elif k == 0:
                for i, speed in enumerate(speeds):
                    part = slice(i * rows, (i + 1) * rows)
                    term[r0 // rows + i, place, 0, sub] = speed * first[part]
                    term[r0 // rows + i, place, 1, sub] = second[part]

        return commit

    def run(body, z, r0, place=None, sub=None):
        pending = None
        for i in range(chunk // block):
            commit = body(z, pl.multiple_of(r0 + i * block, block), place, sub)
            if pending is not None:
                pending()
            pending = commit
        pending()

    def sweep(body, g, span=None):
        low, high = groups[g] if span is None else span

        def turn(i, carry):
            j = i // n_chunks
            place, sub = low + j // 2, lax.rem(j, 2)
            r0 = pl.multiple_of(lax.rem(i, n_chunks) * chunk, chunk)
            run(body, first_layer_of(place) + sub, r0, place, sub)
            return carry

        lax.fori_loop(0, (high - low) * 2 * n_chunks, turn, 0)

    def near_sweep(body, waits=None, sends=None):
        def stripe(c, carry):
            r0 = pl.multiple_of(c * chunk, chunk)
            if waits is not None:
                wait_halo(*waits, c)

            def layer(i, inner_carry):
                run(body, first_layer_of(i // 2) + lax.rem(i, 2), r0)
                return inner_carry

            lax.fori_loop(0, near * 2, layer, 0)
            if sends is not None:
                send_halo(*sends, c)
            return carry

        lax.fori_loop(0, n_chunks, stripe, 0)

    near_sweep(start_adjoint, None, (s0, 4))
    if zs > 1:
        from_z_side(1, 1)
    near_sweep(functools.partial(forward, 0), (q1, 0), (q0, 1))
    for d in range(2, zs):
        from_z_side(1, d)
    middle, rest = (near, near + 1), rounds[1]
    sweep(start_adjoint, 1, middle)
    sweep(functools.partial(forward, 0), 1, middle)
    for d in range(zs):
        from_x_side(1, d)

    def near_adjoint(turn):
        near_sweep(functools.partial(adjoint, STEPS - 1 - turn), (S_[turn % 2], 4 + turn),
                   (S_[(turn + 1) % 2], 5 + turn))

    if doms == 2:
        near_adjoint(0)
    for k in reversed(range(STEPS - 1)):
        inject_moment(k)
    finish_gather(1)
    sweep(start_adjoint, 1, rest)
    if doms != 2:
        near_adjoint(0)
    sweep(functools.partial(forward, 0), 1, rest)
    for turn in range(STEPS - 1):
        k = STEPS - 1 - turn
        if turn > 0:
            near_adjoint(turn)
            sweep(functools.partial(adjoint, k), 1)
        f = turn + 1
        if f + 1 < STEPS:
            near_sweep(functools.partial(forward, f), (Q_[(f + 1) % 2], f), (Q_[f % 2], f + 1))
        if turn == 0:
            sweep(functools.partial(adjoint, k), 1)
        if f + 1 < STEPS:
            sweep(functools.partial(forward, f), 1)

    def sum_copy(g, owner, target, index, landing, send_sem, recv_sem):
        low, high = groups[g]
        places = pl.ds(low, high - low)
        return pltpu.make_async_remote_copy(
            src_ref=term.at[owner, places], dst_ref=landing.at[index, places],
            send_sem=send_sem.at[g, index], recv_sem=recv_sem.at[g, index],
            device_id={"shot": target}, device_id_type=MESH)

    def core_sum(g, j):
        return sum_copy(
            g, 2 * j + (1 - core), shot_at(zi, xi, 1 - core), j, from_core, rc_send, rc_recv)

    def x_sum(g, z):
        return sum_copy(
            g, shot_at(z, 1 - xi, core), shot_at(zi, 1 - xi, core), z, from_x,
            rx_send, rx_recv)

    def z_sum(g, d):
        owner = shot_at(lax.rem(zi + d, zs), xi, core)
        return sum_copy(g, owner, owner, d, from_z, rz_send, rz_recv)

    pairs = chunk // rows // 2

    def last(g):
        low, high = groups[g]

        def stripe(c, carry):
            r0 = pl.multiple_of(c * chunk, chunk)
            if g == 0:
                wait_halo(S_[(STEPS - 1) % 2], 3 + STEPS, c)

            def layer(i, inner_carry):
                place, sub = low + i // 2, lax.rem(i, 2)
                run(functools.partial(adjoint, 0), first_layer_of(place) + sub, r0, place, sub)
                return inner_carry

            lax.fori_loop(0, (high - low) * 2, layer, 0)
            for i in range(pairs):
                core_sum(g, c * pairs + i).start()
            return carry

        lax.fori_loop(0, n_chunks, stripe, 0)

    def add(g, owner, landing, index):
        low, high = groups[g]
        places = pl.ds(low, high - low)
        term[owner, places] = term[owner, places] + landing[index, places]

    order = list(range(1, zs)) + [0]

    def sum_cores(g):
        for x, side in ((1 - xi, True), (xi, False)):
            for d in order:
                z = lax.rem(zi + d, zs)
                j = z * 2 + x
                core_sum(g, j).wait_recv()
                add(g, 2 * j + core, from_core, j)
                if side:
                    x_sum(g, z).start()

    def sum_x(g):
        for d in order:
            z = lax.rem(zi + d, zs)
            x_sum(g, z).wait_recv()
            add(g, shot_at(z, xi, core), from_x, z)
            if d > 0:
                z_sum(g, d).start()

    def sum_z(g):
        low, high = groups[g]
        for d in range(1, zs):
            z_sum(g, d).wait_recv()
        for place in range(low, high):
            total = term[me, place]
            for d in range(1, zs):
                total = total + from_z[d, place]
            pair = pl.ds(first_layer_of(place), 2)
            out[0, pair] = total[0]
            out[1, pair] = total[1]

    sweep(functools.partial(forward, STEPS - 1), 1)
    last(1)
    sum_cores(1)
    near_sweep(functools.partial(forward, STEPS - 1), (Q_[STEPS % 2], STEPS - 1))
    last(0)
    sum_x(1)
    sum_cores(0)
    sum_x(0)
    sum_z(1)
    sum_z(0)
    for g in range(2):
        for j in range(2 * zs):
            core_sum(g, j).wait_send()
        for z in range(zs):
            x_sum(g, z).wait_send()
        for d in range(1, zs):
            z_sum(g, d).wait_send()


def on_device(velocity, epsilon, forward_state, adjoint_state, source_cell, wavelet,
              receiver_cells, residuals, shots, doms):
    depth, width, length = forward_state.shape[2:]
    rows = velocity.shape[1]
    nrec = receiver_cells.shape[1]
    chunk = 64
    zs = shots // 4
    f32 = jnp.float32
    slab = pltpu.VMEM((depth, width, length), f32)
    wide = pltpu.VMEM((depth, length // LANES, width + 2 * PAD, LANES), f32)
    tall = pltpu.VMEM((depth + 4, width, length), f32)
    block = (depth // 2, 2, 2, rows, length)
    dma = pltpu.SemaphoreType.DMA
    scratch = (
        [wide] * 2 + [tall] * 2 + [wide] * 2 + [tall] * 2 + [slab] * 6
        + [slab] * 4 + [slab] * 2 + [slab] * 2
        + [pltpu.VMEM((STEPS, depth, width, length), f32),
           pltpu.VMEM((depth * width, nrec), jnp.bfloat16)]
        + [pltpu.VMEM((shots,) + block, f32), pltpu.VMEM((shots,) + block, f32),
           pltpu.VMEM((2 * zs,) + block, f32), pltpu.VMEM((zs,) + block, f32),
           pltpu.VMEM((zs,) + block, f32)]
        + [dma((6 + 2 * (length // LANES),)), dma((depth // 2, 2)),
           dma((2, zs)), dma((2, zs)), dma((2, 2 * zs)), dma((2, shots)),
           dma((2 * STEPS, 2, width // chunk)), dma((2 * STEPS, 2, width // chunk)),
           dma((2, 2 * zs)), dma((2, 2 * zs)), dma((2, zs)), dma((2, zs)),
           dma((2, zs)), dma((2, zs))]
    )
    vmem = pl.BlockSpec(memory_space=pltpu.VMEM)
    smem = pl.BlockSpec(memory_space=pltpu.SMEM)
    hbm = pl.BlockSpec(memory_space=pl.ANY)
    grads = pl.pallas_call(
        functools.partial(kernel, shots, doms, chunk, 16),
        out_shape=jax.ShapeDtypeStruct((2, depth, rows, length), f32),
        in_specs=[hbm, hbm, hbm, hbm, smem, smem, vmem, vmem],
        out_specs=vmem,
        scratch_shapes=scratch,
        compiler_params=pltpu.CompilerParams(
            collective_id=0, has_side_effects=True, vmem_limit_bytes=56 * 2**20),
        name="vti_window",
    )(velocity, epsilon, forward_state, adjoint_state, source_cell, wavelet,
      receiver_cells, residuals)
    return (grads[0], grads[1])


def solution(mesh):
    placed = (
        P("dom", "shot", None),
        P("dom", "shot", None),
        P("shot", None, "dom", None, None),
        P("shot", None, "dom", None, None),
        P("shot"),
        P("shot", None),
        P("shot", None),
        P("shot", None, None),
    )
    return jax.shard_map(
        functools.partial(on_device, shots=mesh.shape["shot"], doms=mesh.shape["dom"]),
        mesh=mesh,
        in_specs=placed,
        out_specs=(P("dom", "shot", None), P("dom", "shot", None)),
        check_vma=False,
    )
```

```python
import functools

import jax
import jax.numpy as jnp
from jax import lax
from jax.experimental import pallas as pl
from jax.experimental.pallas import tpu as pltpu
from jax.sharding import PartitionSpec as P

STEPS = 4
PAD = 8
LANES = 128
C1, C2 = 4.0 / 3.0, 1.0 / 12.0
MESH = pl.DeviceIdType.MESH


def kernel(
    shots, doms, chunk, block,
    vel, eps, fwd, adj, src, wav, rec, res, out,
    p0, p1, q0, q1, w0, w1, s0, s1, a0, a1, a2, b0, b1, b2,
    flat0, flat1, dep0, dep1, img1, img2, stiff, stretch, inj, hot,
    gath, term, from_core, from_x, from_z,
    load_sem, own_sem, z_send, x_send, c_send, g_recv,
    halo_send, halo_recv, rc_send, rc_recv, rx_send, rx_recv, rz_send, rz_recv,
):
    depth, width, length = stiff.shape
    rows = vel.shape[1]
    nrec = rec.shape[1]
    zs = shots // 4
    me = lax.axis_index("shot")
    dom = lax.axis_index("dom")
    core = lax.rem(me, 2)
    xi = lax.rem(me // 2, 2)
    zi = me // 4
    n_chunks = width // chunk
    n_pairs = depth // 2
    near = 1 if doms == 2 else 2
    groups = ((0, near), (near, n_pairs))

    def shot_at(z, x, c):
        return (z * 2 + x) * 2 + c

    has_low = dom > 0
    has_high = dom < doms - 1

    def first_layer_of(place):
        if doms == 2:
            return 2 * jnp.where(has_low, place, n_pairs - 1 - place)
        end = jnp.where(place == 1, n_pairs - 1, place - 1)
        return 2 * jnp.where(place == 0, 0, end)

    loads = []

    def load(source, target):
        copy = pltpu.make_async_copy(source, target, load_sem.at[len(loads)])
        copy.start()
        loads.append(copy)

    own = []
    for place in range(n_pairs):
        pair = pl.ds(first_layer_of(place), 2)
        for i, model in enumerate((vel, eps)):
            copy = pltpu.make_async_copy(
                model.at[pair], gath.at[me, place, i], own_sem.at[place, i])
            copy.start()
            own.append(copy)
    inner = pl.ds(PAD, width)
    cells = pl.ds(2, depth)
    load(adj.at[0, 1], a1)
    load(adj.at[0, 3], b1)
    tiles = length // LANES
    for t in range(tiles):
        load(fwd.at[0, 1, :, :, pl.ds(t * LANES, LANES)], p1.at[:, t, inner, :])
    load(fwd.at[0, 3], q1.at[cells])
    for t in range(tiles):
        load(fwd.at[0, 0, :, :, pl.ds(t * LANES, LANES)], p0.at[:, t, inner, :])
    load(fwd.at[0, 2], q0.at[cells])
    load(adj.at[0, 0], a0)
    load(adj.at[0, 2], b0)

    barrier = pltpu.get_barrier_semaphore()
    for d in range(1, zs):
        pl.semaphore_signal(
            barrier, inc=1, device_id={"shot": shot_at(lax.rem(zi + d, zs), xi, core)},
            device_id_type=MESH)
    pl.semaphore_signal(
        barrier, inc=1, device_id={"shot": shot_at(zi, 1 - xi, core)}, device_id_type=MESH)
    pl.semaphore_signal(
        barrier, inc=1, device_id={"shot": shot_at(zi, xi, 1 - core)}, device_id_type=MESH)

    @pl.when(has_low)
    def _():
        pl.semaphore_signal(barrier, inc=1, device_id={"dom": dom - 1}, device_id_type=MESH)

    @pl.when(has_high)
    def _():
        pl.semaphore_signal(barrier, inc=1, device_id={"dom": dom + 1}, device_id_type=MESH)

    beside = jnp.where(has_low, 1, 0) + jnp.where(has_high, 1, 0)
    pl.semaphore_wait(barrier, zs + 1 + beside)

    def low_copy(source, field, slot, c):
        stripe = pl.ds(pl.multiple_of(c * chunk, chunk), chunk)
        return pltpu.make_async_remote_copy(
            src_ref=source.at[:, stripe, :], dst_ref=field.at[pl.ds(depth + 2, 2), stripe, :],
            send_sem=halo_send.at[slot, 0, c], recv_sem=halo_recv.at[slot, 1, c],
            device_id={"dom": dom - 1}, device_id_type=MESH)

    def high_copy(source, field, slot, c):
        stripe = pl.ds(pl.multiple_of(c * chunk, chunk), chunk)
        return pltpu.make_async_remote_copy(
            src_ref=source.at[:, stripe, :], dst_ref=field.at[pl.ds(0, 2), stripe, :],
            send_sem=halo_send.at[slot, 1, c], recv_sem=halo_recv.at[slot, 0, c],
            device_id={"dom": dom + 1}, device_id_type=MESH)

    def send_halo(field, slot, c, low=None, high=None):
        low = field.at[pl.ds(2, 2)] if low is None else low
        high = field.at[pl.ds(depth, 2)] if high is None else high

        @pl.when(has_low)
        def _():
            low_copy(low, field, slot, c).start()

        @pl.when(has_high)
        def _():
            high_copy(high, field, slot, c).start()

    def wait_halo(field, slot, c):
        low, high = field.at[pl.ds(2, 2)], field.at[pl.ds(depth, 2)]

        @pl.when(has_low)
        def _():
            low_copy(low, field, slot, c).wait_send()
            high_copy(high, field, slot, c).wait_recv()

        @pl.when(has_high)
        def _():
            high_copy(high, field, slot, c).wait_send()
            low_copy(low, field, slot, c).wait_recv()

    for c in range(n_chunks):
        send_halo(
            q1, 0, c, fwd.at[0, 3, pl.ds(0, 2)], fwd.at[0, 3, pl.ds(depth - 2, 2)])

    def block_copy(g, owner, target, send_sem):
        low, high = groups[g]
        part = gath.at[owner, pl.ds(low, high - low)]
        return pltpu.make_async_remote_copy(
            src_ref=part, dst_ref=part, send_sem=send_sem, recv_sem=g_recv.at[g, owner],
            device_id={"shot": target}, device_id_type=MESH)

    def to_x(g, z):
        return block_copy(
            g, shot_at(z, xi, core), shot_at(zi, 1 - xi, core), x_send.at[g, z])

    def to_core(g, z, x):
        return block_copy(
            g, shot_at(z, x, core), shot_at(zi, xi, 1 - core), c_send.at[g, z * 2 + x])

    def to_z(g, d):
        return block_copy(
            g, me, shot_at(lax.rem(zi + d, zs), xi, core), z_send.at[g, d])

    def arrived(g, owner):
        block_copy(g, owner, me, x_send.at[g, 0]).wait_recv()

    def from_z_side(g, d):
        other = lax.rem(zi + (zs - d), zs)
        arrived(g, shot_at(other, xi, core))
        to_x(g, other).start()
        to_core(g, other, xi).start()

    def from_x_side(g, d):
        other = lax.rem(zi + (zs - d), zs)
        arrived(g, shot_at(other, 1 - xi, core))
        to_core(g, other, 1 - xi).start()

    def finish_gather(g):
        for z in range(zs):
            for x in range(2):
                arrived(g, shot_at(z, x, 1 - core))
        for d in range(1, zs):
            to_z(g, d).wait_send()
        for z in range(zs):
            to_x(g, z).wait_send()
            for x in range(2):
                to_core(g, z, x).wait_send()

        def spread(place, carry):
            pair = pl.ds(first_layer_of(place), 2)
            for s in range(shots):
                part = slice(s * rows, (s + 1) * rows)
                speed = gath[s, place, 0]
                stiff[pair, part, :] = speed * speed
                stretch[pair, part, :] = 1.0 + 2.0 * gath[s, place, 1]
            return carry

        lax.fori_loop(*groups[g], spread, 0)

    for copy in own:
        copy.wait()
    for g in range(2):
        to_x(g, zi).start()
        for d in range(1, zs):
            to_z(g, d).start()
        to_core(g, zi, xi).start()

    edge = jnp.zeros((depth, tiles, PAD, LANES), jnp.float32)
    for field in (p0, p1, w0, w1):
        field[:, :, 0:PAD, :] = edge
        field[:, :, PAD + width:PAD + width + PAD, :] = edge
    halo = jnp.zeros((2, width, length), jnp.float32)

    @pl.when(dom == 0)
    def _():
        for field in (q0, q1, s0, s1):
            field[0:2] = halo

    @pl.when(dom == doms - 1)
    def _():
        for field in (q0, q1, s0, s1):
            field[depth + 2:depth + 4] = halo

    first_row = dom * (depth * width)
    rec_row = rec[...] // length - first_row
    rec_col = lax.rem(rec[...], length)
    all_rows = depth * width

    def fill_hot(z, carry):
        ids = lax.broadcasted_iota(jnp.int32, (width, nrec), 0) + z * width
        hot[pl.ds(pl.multiple_of(z * width, width), width), :] = jnp.where(
            ids == rec_row, 1.0, 0.0).astype(jnp.bfloat16)
        return carry

    span = depth // 2

    def inject_moment(k):
        col_hit = lax.broadcasted_iota(jnp.int32, (length, nrec), 0) == rec_col
        amount = res[0, k:k + 1, :]
        parts = []
        for _ in range(3):
            part = amount.astype(jnp.bfloat16).astype(jnp.float32)
            parts.append(jnp.where(col_hit, part, 0.0).astype(jnp.bfloat16))
            amount = amount - part

        def fill(i, carry):
            here = hot[pl.ds(pl.multiple_of(i * span * width, width), span * width), :]
            total = None
            for part in parts:
                product = lax.dot_general(
                    here, part, (((1,), (1,)), ((), ())),
                    preferred_element_type=jnp.float32)
                total = product if total is None else total + product
            inj[k, pl.ds(i * span, span)] = total.reshape(span, width, length)
            return carry

        lax.fori_loop(0, depth // span, fill, 0)

    lax.fori_loop(0, depth, fill_hot, 0)
    inject_moment(STEPS - 1)
    for d in range(1, zs):
        from_z_side(0, d)
    for d in range(zs):
        from_x_side(0, d)
    for copy in loads:
        copy.wait()
    finish_gather(0)

    lane = lax.broadcasted_iota(jnp.int32, (block, LANES), 1)

    def lateral(field, z, r0):
        def at(t, offset):
            return field[z, t, pl.ds(r0 + (PAD + offset), block), :]

        centre = [at(t, 0) for t in range(tiles)]

        def shifted(amount):
            turned = [pltpu.roll(t, amount % LANES, 1) for t in centre]
            result = []
            for i in range(tiles):
                if amount > 0:
                    fill = turned[i - 1] if i > 0 else 0.0
                    result.append(jnp.where(lane >= amount, turned[i], fill))
                else:
                    fill = turned[i + 1] if i + 1 < tiles else 0.0
                    result.append(jnp.where(lane < LANES + amount, turned[i], fill))
            return result

        up1, down1, up2, down2 = shifted(1), shifted(-1), shifted(2), shifted(-2)
        result = []
        for t in range(tiles):
            close = (up1[t] + down1[t]) + (at(t, 1) + at(t, -1))
            remote = (up2[t] + down2[t]) + (at(t, 2) + at(t, -2))
            result.append(C1 * close - C2 * remote - 5.0 * centre[t])
        return jnp.concatenate(centre, axis=1), jnp.concatenate(result, axis=1)

    def get_tiles(field, z, r0):
        return jnp.concatenate(
            [field[z, t, pl.ds(r0 + PAD, block), :] for t in range(tiles)], axis=1)

    def put_tiles(field, z, r0, value):
        for t in range(tiles):
            field[z, t, pl.ds(r0 + PAD, block), :] = value[:, t * LANES:(t + 1) * LANES]

    def vertical(field, z, r0):
        def at(offset):
            return field[z + (2 + offset), pl.ds(r0, block), :]

        centre = at(0)
        return centre, C1 * (at(1) + at(-1)) - C2 * (at(2) + at(-2)) - 2.5 * centre

    source_row = src[0] // length - first_row
    source_col = lax.rem(src[0], length)
    row_ids = lax.broadcasted_iota(jnp.int32, (block, length), 0)
    col_hit = lax.broadcasted_iota(jnp.int32, (1, length), 1) == source_col
    P_, Q_ = (p0, p1), (q0, q1)
    W_, S_ = (w0, w1), (s0, s1)

    def forward(k, z, r0, place=None, sub=None):
        now, old = (k + 1) % 2, k % 2
        here = (z, pl.ds(r0, block), slice(None))
        p_now, flat = lateral(P_[now], z, r0)
        q_now, dep = vertical(Q_[now], z, r0)
        if k + 1 < STEPS:
            st, sr = stiff[here], stretch[here]
            pulse = jnp.where(
                row_ids == source_row - (z * width + r0),
                jnp.where(col_hit, wav[0, k], 0.0), 0.0)
            layer = (z + 2, pl.ds(r0, block), slice(None))
            p_old, q_old = get_tiles(P_[old], z, r0), Q_[old][layer]
            p_new = 2.0 * p_now - p_old + st * (sr * flat + dep) + pulse
            q_new = 2.0 * q_now - q_old + st * (flat + dep) + pulse
        if k >= 2:
            a, b = (a1[here], b1[here]) if k == 2 else (a0[here], b0[here])
            one, two = a * flat, a * dep + b * (flat + dep)
            if k > 2:
                one, two = img1[here] + one, img2[here] + two

        def commit():
            if k + 1 < STEPS:
                put_tiles(P_[old], z, r0, p_new)
                Q_[old][layer] = q_new
            if k == 0:
                flat0[here], dep0[here] = flat, dep
            elif k == 1:
                flat1[here], dep1[here] = flat, dep
            else:
                img1[here], img2[here] = one, two

        return commit

    def weigh(slot, z, r0, a, b):
        here = (z, pl.ds(r0, block), slice(None))
        st, sr = stiff[here], stretch[here]
        weighed, plain = st * (sr * a + b), st * (a + b)

        def commit():
            put_tiles(W_[slot], z, r0, weighed)
            S_[slot][z + 2, pl.ds(r0, block), :] = plain

        return commit

    def start_adjoint(z, r0, place=None, sub=None):
        here = (z, pl.ds(r0, block), slice(None))
        return weigh(0, z, r0, a1[here], b1[here])

    def adjoint(k, z, r0, place=None, sub=None):
        turn = STEPS - 1 - k
        old_a, now_a, new_a = ((a0, a1, a0), (a1, a0, a1), (a0, a1, a2), (a1, a2, None))[turn]
        old_b, now_b, new_b = ((b0, b1, b0), (b1, b0, b1), (b0, b1, b2), (b1, b2, None))[turn]
        here = (z, pl.ds(r0, block), slice(None))
        a = 2.0 * now_a[here] - old_a[here] + lateral(W_[turn % 2], z, r0)[1] + inj[(k,) + here]
        b = 2.0 * now_b[here] - old_b[here] + vertical(S_[turn % 2], z, r0)[1]
        commit_weighed = None
        if new_a is not None:
            commit_weighed = weigh((turn + 1) % 2, z, r0, a, b)
        if k == 1:
            flat, dep = flat1[here], dep1[here]
            one = img1[here] + a * flat
            two = img2[here] + (a * dep + b * (flat + dep))
        elif k == 0:
            flat, dep = flat0[here], dep0[here]
            one = img1[here] + a * flat
            two = img2[here] + (a * dep + b * (flat + dep))
            st, sr = stiff[here], stretch[here]
            first = 2.0 * (sr * one + two)
            second = 2.0 * st * one
            speeds = [gath[r0 // rows + i, place, 0, sub] for i in range(block // rows)]

        def commit():
            if new_a is not None:
                new_a[here], new_b[here] = a, b
                commit_weighed()
            if k == 1:
                img1[here], img2[here] = one, two
            elif k == 0:
                for i, speed in enumerate(speeds):
                    part = slice(i * rows, (i + 1) * rows)
                    term[r0 // rows + i, place, 0, sub] = speed * first[part]
                    term[r0 // rows + i, place, 1, sub] = second[part]

        return commit

    def row_of(r0, offset):
        return offset if isinstance(r0, int) else pl.multiple_of(r0 + offset, block)

    def run(body, z, r0, place=None, sub=None, size=chunk):
        pending = None
        for i in range(size // block):
            commit = body(z, row_of(r0, i * block), place, sub)
            if pending is not None:
                pending()
            pending = commit
        pending()

    def sweep(body, g):
        low, high = groups[g]

        def turn(i, carry):
            place, sub = low + i // 2, lax.rem(i, 2)
            run(body, first_layer_of(place) + sub, 0, place, sub, width)
            return carry

        lax.fori_loop(0, (high - low) * 2, turn, 0)

    def near_sweep(body, waits=None, sends=None):
        def stripe(c, carry):
            r0 = pl.multiple_of(c * chunk, chunk)
            if waits is not None:
                wait_halo(*waits, c)

            def layer(i, inner_carry):
                run(body, first_layer_of(i // 2) + lax.rem(i, 2), r0)
                return inner_carry

            lax.fori_loop(0, near * 2, layer, 0)
            if sends is not None:
                send_halo(*sends, c)
            return carry

        lax.fori_loop(0, n_chunks, stripe, 0)

    near_sweep(start_adjoint, None, (s0, 4))
    if zs > 1:
        from_z_side(1, 1)
    near_sweep(functools.partial(forward, 0), (q1, 0), (q0, 1))
    for d in range(2, zs):
        from_z_side(1, d)
    inject_moment(2)
    inject_moment(1)
    for d in range(zs):
        from_x_side(1, d)
    inject_moment(0)
    finish_gather(1)
    sweep(start_adjoint, 1)
    sweep(functools.partial(forward, 0), 1)
    for turn in range(STEPS - 1):
        k = STEPS - 1 - turn
        near_sweep(functools.partial(adjoint, k), (S_[turn % 2], 4 + turn),
                   (S_[(turn + 1) % 2], 5 + turn))
        sweep(functools.partial(adjoint, k), 1)
        f = turn + 1
        if f + 1 < STEPS:
            near_sweep(functools.partial(forward, f), (Q_[(f + 1) % 2], f), (Q_[f % 2], f + 1))
            sweep(functools.partial(forward, f), 1)

    def sum_copy(g, owner, target, index, landing, send_sem, recv_sem):
        low, high = groups[g]
        places = pl.ds(low, high - low)
        return pltpu.make_async_remote_copy(
            src_ref=term.at[owner, places], dst_ref=landing.at[index, places],
            send_sem=send_sem.at[g, index], recv_sem=recv_sem.at[g, index],
            device_id={"shot": target}, device_id_type=MESH)

    def core_sum(g, j):
        return sum_copy(
            g, 2 * j + (1 - core), shot_at(zi, xi, 1 - core), j, from_core, rc_send, rc_recv)

    def x_sum(g, z):
        return sum_copy(
            g, shot_at(z, 1 - xi, core), shot_at(zi, 1 - xi, core), z, from_x,
            rx_send, rx_recv)

    def z_sum(g, d):
        owner = shot_at(lax.rem(zi + d, zs), xi, core)
        return sum_copy(g, owner, owner, d, from_z, rz_send, rz_recv)

    pairs = chunk // rows // 2

    def last(g):
        low, high = groups[g]

        def stripe(c, carry):
            r0 = pl.multiple_of(c * chunk, chunk)
            if g == 0:
                wait_halo(S_[(STEPS - 1) % 2], 3 + STEPS, c)

            def layer(i, inner_carry):
                place, sub = low + i // 2, lax.rem(i, 2)
                run(functools.partial(adjoint, 0), first_layer_of(place) + sub, r0, place, sub)
                return inner_carry

            lax.fori_loop(0, (high - low) * 2, layer, 0)
            for i in range(pairs):
                core_sum(g, c * pairs + i).start()
            return carry

        lax.fori_loop(0, n_chunks, stripe, 0)

    def add(g, owner, landing, index):
        low, high = groups[g]
        places = pl.ds(low, high - low)
        term[owner, places] = term[owner, places] + landing[index, places]

    order = list(range(1, zs)) + [0]

    def sum_cores(g):
        for x, side in ((1 - xi, True), (xi, False)):
            for d in order:
                z = lax.rem(zi + d, zs)
                j = z * 2 + x
                core_sum(g, j).wait_recv()
                add(g, 2 * j + core, from_core, j)
                if side:
                    x_sum(g, z).start()

    def sum_x(g):
        for d in order:
            z = lax.rem(zi + d, zs)
            x_sum(g, z).wait_recv()
            add(g, shot_at(z, xi, core), from_x, z)
            if d > 0:
                z_sum(g, d).start()

    def sum_z(g):
        low, high = groups[g]
        for d in range(1, zs):
            z_sum(g, d).wait_recv()
        for place in range(low, high):
            total = term[me, place]
            for d in range(1, zs):
                total = total + from_z[d, place]
            pair = pl.ds(first_layer_of(place), 2)
            out[0, pair] = total[0]
            out[1, pair] = total[1]

    sweep(functools.partial(forward, STEPS - 1), 1)
    last(1)
    sum_cores(1)
    near_sweep(functools.partial(forward, STEPS - 1), (Q_[STEPS % 2], STEPS - 1))
    last(0)
    sum_x(1)
    sum_cores(0)
    sum_x(0)
    sum_z(1)
    sum_z(0)
    for g in range(2):
        for j in range(2 * zs):
            core_sum(g, j).wait_send()
        for z in range(zs):
            x_sum(g, z).wait_send()
        for d in range(1, zs):
            z_sum(g, d).wait_send()


def on_device(velocity, epsilon, forward_state, adjoint_state, source_cell, wavelet,
              receiver_cells, residuals, shots, doms):
    depth, width, length = forward_state.shape[2:]
    rows = velocity.shape[1]
    nrec = receiver_cells.shape[1]
    chunk = 64
    zs = shots // 4
    f32 = jnp.float32
    slab = pltpu.VMEM((depth, width, length), f32)
    wide = pltpu.VMEM((depth, length // LANES, width + 2 * PAD, LANES), f32)
    tall = pltpu.VMEM((depth + 4, width, length), f32)
    block = (depth // 2, 2, 2, rows, length)
    dma = pltpu.SemaphoreType.DMA
    scratch = (
        [wide] * 2 + [tall] * 2 + [wide] * 2 + [tall] * 2 + [slab] * 6
        + [slab] * 4 + [slab] * 2 + [slab] * 2
        + [pltpu.VMEM((STEPS, depth, width, length), f32),
           pltpu.VMEM((depth * width, nrec), jnp.bfloat16)]
        + [pltpu.VMEM((shots,) + block, f32), pltpu.VMEM((shots,) + block, f32),
           pltpu.VMEM((2 * zs,) + block, f32), pltpu.VMEM((zs,) + block, f32),
           pltpu.VMEM((zs,) + block, f32)]
        + [dma((6 + 2 * (length // LANES),)), dma((depth // 2, 2)),
           dma((2, zs)), dma((2, zs)), dma((2, 2 * zs)), dma((2, shots)),
           dma((2 * STEPS, 2, width // chunk)), dma((2 * STEPS, 2, width // chunk)),
           dma((2, 2 * zs)), dma((2, 2 * zs)), dma((2, zs)), dma((2, zs)),
           dma((2, zs)), dma((2, zs))]
    )
    vmem = pl.BlockSpec(memory_space=pltpu.VMEM)
    smem = pl.BlockSpec(memory_space=pltpu.SMEM)
    hbm = pl.BlockSpec(memory_space=pl.ANY)
    grads = pl.pallas_call(
        functools.partial(kernel, shots, doms, chunk, 16),
        out_shape=jax.ShapeDtypeStruct((2, depth, rows, length), f32),
        in_specs=[hbm, hbm, hbm, hbm, smem, smem, vmem, vmem],
        out_specs=vmem,
        scratch_shapes=scratch,
        compiler_params=pltpu.CompilerParams(
            collective_id=0, has_side_effects=True, vmem_limit_bytes=56 * 2**20),
        name="vti_window",
    )(velocity, epsilon, forward_state, adjoint_state, source_cell, wavelet,
      receiver_cells, residuals)
    return (grads[0], grads[1])


def solution(mesh):
    placed = (
        P("dom", "shot", None),
        P("dom", "shot", None),
        P("shot", None, "dom", None, None),
        P("shot", None, "dom", None, None),
        P("shot"),
        P("shot", None),
        P("shot", None),
        P("shot", None, None),
    )
    return jax.shard_map(
        functools.partial(on_device, shots=mesh.shape["shot"], doms=mesh.shape["dom"]),
        mesh=mesh,
        in_specs=placed,
        out_specs=(P("dom", "shot", None), P("dom", "shot", None)),
        check_vma=False,
    )
```
